128 devices in a mesh: lon: 16 (over z, x_hi, core), lat: 8 (over x_lo, y).
Axes of the slice: x: 4 (x_hi: 2, x_lo: 2; x = x_hi * 2 + x_lo), y: 4, z: 4, core: 2. Of those that a mesh axis runs over, the one named last changes fastest.
Arguments:
- adjoint_end: float32 [4, 32, 32, 2048], P(None, None, 'lat', 'lon'), may hold values from -6 to 6
- face_courant: bfloat16 [4, 4, 32, 32, 2048], P(None, None, None, 'lat', 'lon'), may hold values from 0.019897461 to 0.22949219
- mixing: bfloat16 [31, 32, 2048], P(None, 'lat', 'lon'), may hold values from 0.019897461 to 0.19921875
- row_shift: int32 [4, 32], P(None, 'lat'), may hold values from 0 to 2047, as said below
- tile_jac: float32 [128, 4, 128, 8, 128], P(('lon', 'lat')), may hold values from -6 to 6
- tile_cell: int32 [128, 4, 128, 8], P(('lon', 'lat')), may hold values from 0 to 511
- tile_count: int32 [128, 4, 128], P(('lon', 'lat')), may hold values from 1 to 8, as said below
Outputs:
- adjoint_start: float32 [4, 32, 32, 2048], P(None, None, 'lat', 'lon')
- flux_sensitivity: float32 [4, 32, 2048], P(None, 'lat', 'lon')
The draws below stay inside these ranges and needn't reach their ends.
Inputs may be any that keep to these rules, and one draw needn't show every extreme that they name: `row_shift`: row j's shift is below max(2048 // (1 + min(j, 31 - j)), 2) at every step and equals that bound minus one at some step; the first row's shift is 2047 at every step. `tile_cell`: cell index row * 128 + column within the owner's block. `tile_count`: slots 0 to count - 1 of a tile hold soundings; the rest are padding. At every step some owner receives 8 soundings from every device.
All inputs are finite; a program needn't handle non-finite values.
Results may differ from the reference program's by a relative error of at most 0.0003.
Values sent between devices are 32-bit elements; how exact they have to be, the bound alone decides.
A program may use at most 128 MiB of HBM per device.

```python
import math
import jax
import jax.numpy as jnp

TRACERS = 4
LEVELS = 32
LAT_DEV = 4
LON_DEV = 128
STEPS = 4
SLOTS = 8
NLAT = 32
NLON = 2048
OWNERS = 128
N_LAT = 8


def draw_row_shift(key, part):
    key = jax.random.fold_in(key, 11)
    rows = jnp.arange(NLAT, dtype=jnp.int32)
    from_pole = jnp.minimum(rows, NLAT - 1 - rows)
    limits = jnp.maximum(NLON // (1 + from_pole), 2)
    drawn = jax.random.randint(key, (STEPS, NLAT), 0, limits[None, :])
    step_ids = jnp.arange(STEPS, dtype=jnp.int32)
    at_bound = step_ids[:, None] == (rows % STEPS)[None, :]
    drawn = jnp.where(at_bound, limits[None, :] - 1, drawn)
    return jnp.where(rows[None, :] == 0, NLON - 1, drawn).astype(jnp.int32)


def draw_tile_count(key, part):
    key = jax.random.fold_in(key, 17)
    first_key, second_key = jax.random.split(key)
    counts = jax.random.randint(first_key, (OWNERS, STEPS, OWNERS), 1, SLOTS + 1)
    busiest = jax.random.randint(second_key, (STEPS,), 0, OWNERS)
    owner_ids = jnp.arange(OWNERS, dtype=jnp.int32)
    filled = owner_ids[None, None, :] == busiest[None, :, None]
    return jnp.where(filled, SLOTS, counts).astype(jnp.int32)


def set_ends(entries, own_key, least, top_value):
    spot = [jax.random.randint(jax.random.fold_in(own_key, axis), (), 0, length) for axis, length in enumerate(entries.shape)]
    longest = entries.shape.index(max(entries.shape))
    neighbour = spot[:longest] + [(spot[longest] + 1) % entries.shape[longest]] + spot[longest + 1:]
    return entries.at[tuple(spot)].set(least).at[tuple(neighbour)].set(top_value)


def level_of(own_key, extent, cuts, low, high):
    def one(dim, shards_of):
        heights = jax.random.uniform(jax.random.fold_in(jax.random.fold_in(own_key, 6), dim), (shards_of,), jnp.float32, low / len(cuts), high / len(cuts))
        return jnp.repeat(jnp.exp(heights), extent[dim] // shards_of).reshape((-1,) + (1,) * (len(extent) - dim - 1))

    level = one(*cuts[0])
    for cut in cuts[1:]:
        level = level * one(*cut)
    return level


def centred(stream_key, shape, deviation, most, cuts=(), kind=jnp.bfloat16):
    result = jax.random.normal(stream_key, shape, jnp.float32) * deviation
    if len(cuts) > 0:
        result = level_of(stream_key, shape, cuts, -0.22, 0.18) * result
    return jnp.clip(result, min=-most, max=most).astype(kind)


def setup_inputs(seed: int = 0) -> dict:
    streams_of = jax.random.split(jax.random.key(seed), 8)
    return {
        "adjoint_end": centred(streams_of[0], (TRACERS, LEVELS, NLAT, NLON), 1.0, 6.0, ((2, 8), (3, 16)), jnp.float32),
        "face_courant": jnp.clip(jnp.exp(math.log(0.22949219) - 2.4452768550172324 * jax.random.uniform(streams_of[1], (4, STEPS, LEVELS, NLAT, NLON), jnp.float32) ** level_of(streams_of[1], (4, STEPS, LEVELS, NLAT, NLON), ((3, 8), (4, 16)), -0.2, 0.2)), 0.019897461, 0.22949219).astype(jnp.bfloat16),
        "mixing": jnp.clip(jnp.exp(math.log(0.19921875) - 2.3038113 * jax.random.uniform(streams_of[2], (LEVELS - 1, NLAT, NLON), jnp.float32) ** level_of(streams_of[2], (LEVELS - 1, NLAT, NLON), ((1, 8), (2, 16)), -0.2, 0.2)), 0.019897461, 0.19921875).astype(jnp.bfloat16),
        "row_shift": draw_row_shift(jax.random.fold_in(streams_of[7], 71), 0),
        "tile_jac": centred(streams_of[4], (OWNERS, STEPS, OWNERS, SLOTS, TRACERS * LEVELS), 1.0, 6.0, ((0, 128),), jnp.float32),
        "tile_cell": set_ends(jax.random.randint(streams_of[5], (OWNERS, STEPS, OWNERS, SLOTS), 0, LAT_DEV * LON_DEV), jax.random.fold_in(streams_of[5], 1), 0, (LAT_DEV * LON_DEV) - 1).astype(jnp.int32),
        "tile_count": draw_tile_count(jax.random.fold_in(streams_of[7], 71), 0),
    }


def forcing_field(jac_step, cell_step, count_step):
    slot_ids = jnp.arange(SLOTS, dtype=jnp.int32)
    live = (slot_ids[None, None, :] < count_step[:, :, None]).astype(jnp.float32)
    owner_ids = jnp.arange(OWNERS, dtype=jnp.int32)
    lon_owner = owner_ids // N_LAT
    lat_owner = owner_ids % N_LAT
    row_index = lat_owner[None, :, None] * LAT_DEV + cell_step // LON_DEV
    col_index = lon_owner[None, :, None] * LON_DEV + cell_step % LON_DEV
    flat_index = (row_index * NLON + col_index).reshape(-1).astype(jnp.int32)
    values = (jac_step * live[..., None]).reshape(-1, TRACERS * LEVELS)
    total = jnp.zeros((NLAT * NLON, TRACERS * LEVELS), jnp.float32).at[flat_index].add(values)
    return total.T.reshape(TRACERS, LEVELS, NLAT, NLON)


def mix_levels(summed, mixing):
    rates = mixing.astype(jnp.float32)[None]
    fluxes = rates * (summed[:, 1:] - summed[:, :-1])
    zero_layer = jnp.zeros_like(summed[:, :1])
    return summed + jnp.concatenate([fluxes, zero_layer], axis=1) - jnp.concatenate([zero_layer, fluxes], axis=1)


def roll_rows(mixed, shifts):
    columns = jnp.arange(NLON, dtype=jnp.int32)
    source = (columns[None, :] + shifts[:, None]) % NLON
    source = jnp.broadcast_to(source[None, None], mixed.shape).astype(jnp.int32)
    return jnp.take_along_axis(mixed, source, axis=3)


def transport(rolled, courant):
    to_north = courant[0].astype(jnp.float32)
    to_south = courant[1].astype(jnp.float32)
    to_east = courant[2].astype(jnp.float32)
    to_west = courant[3].astype(jnp.float32)
    zero_row = jnp.zeros_like(rolled[:, :, :1])
    above_row = jnp.concatenate([rolled[:, :, 1:], zero_row], axis=2)
    below_row = jnp.concatenate([zero_row, rolled[:, :, :-1]], axis=2)
    east_cell = jnp.roll(rolled, -1, axis=3)
    west_cell = jnp.roll(rolled, 1, axis=3)
    return (rolled + to_north * (above_row - rolled) + to_south * (below_row - rolled)
            + to_east * (east_cell - rolled) + to_west * (west_cell - rolled))


def reference(adjoint_end, face_courant, mixing, row_shift, tile_jac, tile_cell, tile_count):
    adjoint = adjoint_end
    flux_sensitivity = jnp.zeros((TRACERS, NLAT, NLON), jnp.float32)
    for time_step in range(STEPS - 1, -1, -1):
        summed = adjoint + forcing_field(tile_jac[:, time_step], tile_cell[:, time_step], tile_count[:, time_step])
        mixed = mix_levels(summed, mixing)
        rolled = roll_rows(mixed, row_shift[time_step])
        adjoint = transport(rolled, face_courant[:, time_step])
        flux_sensitivity = flux_sensitivity + adjoint[:, 0]
    return adjoint, flux_sensitivity
```

```python
import functools

import jax
import jax.numpy as jnp
from jax import lax
from jax.experimental import pallas as pl
from jax.experimental.pallas import tpu as pltpu
from jax.sharding import PartitionSpec as P

MESH = pl.DeviceIdType.MESH
F32 = jnp.float32
N_LON = 16
N_LAT = 8
N_DEV = N_LON * N_LAT
SHIFT_LANE = 32


def lon_of_group(g):
    k = g // 2
    x_hi = k // 4
    z = k + x_hi * (7 - 2 * k)
    return z * 4 + x_hi * 2 + g % 2


def group_of_lon(lon):
    z = lon // 4
    k = z + (lon // 2) % 2 * (7 - 2 * z)
    return k * 2 + lon % 2


def remote(src, dst, send_sem, recv_sem, lon, lat):
    return pltpu.make_async_remote_copy(
        src_ref=src,
        dst_ref=dst,
        send_sem=send_sem,
        recv_sem=recv_sem,
        device_id=(lon, lat),
        device_id_type=MESH,
    )


def wait_bytes(ref, sem):
    pltpu.make_async_copy(ref, ref, sem).wait()


def kernel(
    adj, courant, mixing, jac, note,
    out, flux_out,
    jac_in, note_in, shifts, forcing, padded, rates, mixed, edges, courant_out,
    inbox, halo, courant_in, rates_in, rates_t, state, twice, rolled, final, final_out, flux, flux_send,
    js, jr, ns, nr, ps, pr, fs, fr, ks, kr, rs, rr, es, er, os, orv, xs, xr, sm,
):
    lon, lat = lax.axis_index("lon"), lax.axis_index("lat")
    me = lon * N_LAT + lat
    g = group_of_lon(lon)
    north, south = lax.rem(lat + N_LAT - 1, N_LAT), lax.rem(lat + 1, N_LAT)
    lon_up, lon_down = lon_of_group(lax.rem(g + 1, N_LON)), lon_of_group(lax.rem(g + N_LON - 1, N_LON))

    barrier = pltpu.get_barrier_semaphore()

    def peer(k):
        return lax.rem(lon + k // N_LAT, N_LON), lax.rem(lat + k % N_LAT, N_LAT)

    def greet(k, carry):
        pl.semaphore_signal(barrier, inc=1, device_id=peer(k), device_id_type=MESH)
        return carry

    lax.fori_loop(1, N_DEV, greet, 0)
    pl.semaphore_wait(barrier, N_DEV - 1)

    def send_tiles(t, notes):
        def body(k, carry):
            p_lon, p_lat = peer(k)
            owner = p_lon * N_LAT + p_lat
            if notes:
                remote(note.at[pl.ds(owner, 1)], note_in.at[pl.ds(me, 1)], ns, nr, p_lon, p_lat).start()
            remote(
                jac.at[t, pl.ds(owner * 8, 8)], jac_in.at[t, pl.ds(me * 8, 8)], js.at[t], jr.at[t], p_lon, p_lat
            ).start()
            return carry

        if notes:
            pltpu.make_async_copy(note.at[pl.ds(me, 1)], note_in.at[pl.ds(me, 1)], nr).start()
        pltpu.make_async_copy(jac.at[t, pl.ds(me * 8, 8)], jac_in.at[t, pl.ds(me * 8, 8)], jr.at[t]).start()
        lax.fori_loop(1, N_DEV, body, 0)

    def to_groups(send):
        def body(k, carry):
            target = lax.rem(lon + k, N_LON)
            send(group_of_lon(target), target)
            return carry

        lax.fori_loop(1, N_LON, body, 0)

    def send_blocks(src, dst, send_sem, recv_sem):
        pltpu.make_async_copy(src.at[pl.ds(g * 32, 32)], dst.at[pl.ds(lon * 32, 32)], recv_sem).start()

        def one(to, target):
            remote(
                src.at[pl.ds(to * 32, 32)], dst.at[pl.ds(lon * 32, 32)], send_sem, recv_sem, target, lat
            ).start()

        to_groups(one)

    def convert_courant(t):
        for face in range(4):
            values = courant[face, t].astype(F32).reshape(128, 128)
            for to in range(N_LON):
                courant_out[t, pl.ds(to * 32 + face * 8, 8)] = values[to * 8 : to * 8 + 8]

    def scatter(t):
        cells = jnp.transpose(note_in[...].astype(F32))
        cell_ids = lax.broadcasted_iota(jnp.int32, (512, 128), 0).astype(F32)
        total = jnp.zeros((512, 256), F32)
        for pair in range(4):
            hot, value = [], []
            for slot in (2 * pair, 2 * pair + 1):
                row = cells[t * 8 + slot : t * 8 + slot + 1]
                hot.append(jnp.where(cell_ids == row, 1.0, 0.0).astype(jnp.bfloat16))
                x = jac_in[t, pl.ds(slot, 128, stride=8)]
                high = x.astype(jnp.bfloat16)
                low = (x - high.astype(F32)).astype(jnp.bfloat16)
                value.append(jnp.concatenate([high, low], axis=1))
            total = total + jnp.dot(
                jnp.concatenate(hot, axis=1), jnp.concatenate(value, axis=0), preferred_element_type=F32
            )
        both = total[:, :128] + total[:, 128:]
        for row in range(4):
            by_entry = jnp.transpose(both[row * 128 : row * 128 + 128])
            for c in range(4):
                forcing[c, pl.ds(row, 32, stride=4)] = by_entry[c * 32 : c * 32 + 32]

    send_tiles(3, True)

    convert_courant(3)
    send_blocks(courant_out.at[3], courant_in.at[3], ks.at[1], kr.at[1])
    rates[...] = jnp.zeros_like(rates)
    rates[pl.ds(8, 124)] = mixing[...].astype(F32).reshape(124, 128)
    send_tiles(2, False)

    wait_bytes(note_in, nr)
    for i, row in enumerate((north, lat, south)):
        pltpu.make_async_copy(note_in.at[pl.ds(lon * N_LAT + row, 1)], shifts.at[pl.ds(i, 1)], sm.at[i]).start()
    wait_bytes(jac_in.at[3], jr.at[3])
    scatter(3)

    padded[...] = jnp.zeros_like(padded)
    for c in range(4):
        padded[c, pl.ds(8, 128)] = adj[c] + forcing[c]
        mid, above, below = padded[c, pl.ds(8, 128)], padded[c, pl.ds(12, 128)], padded[c, pl.ds(4, 128)]
        value = mid + rates[pl.ds(8, 128)] * (above - mid) - rates[pl.ds(4, 128)] * (mid - below)
        for to in range(N_LON):
            mixed[3, pl.ds(to * 32 + c * 8, 8)] = value[to * 8 : to * 8 + 8]
        padded[c, pl.ds(8, 128)] = value
        edges[0, pl.ds(c, 32, stride=4)] = padded[c, pl.ds(8, 32, stride=4)]
        edges[1, pl.ds(c, 32, stride=4)] = padded[c, pl.ds(11, 32, stride=4)]
    send_blocks(mixed.at[3], inbox.at[3], ps.at[0], pr.at[0])

    def send_edges(k, carry):
        target = lax.rem(lon + k, N_LON)
        to = group_of_lon(target)
        remote(
            edges.at[1, pl.ds(to * 8, 8)], halo.at[0, pl.ds(lon * 8, 8)], ps.at[1], pr.at[1], target, south
        ).start()
        remote(
            edges.at[0, pl.ds(to * 8, 8)], halo.at[1, pl.ds(lon * 8, 8)], ps.at[2], pr.at[2], target, north
        ).start()
        return carry

    lax.fori_loop(0, N_LON, send_edges, 0)

    def make_forcing(t):
        wait_bytes(jac_in.at[t], jr.at[t])
        scatter(t)
        for c in range(4):
            for to in range(N_LON):
                mixed[t, pl.ds(to * 32 + c * 8, 8)] = forcing[c, pl.ds(to * 8, 8)]
        send_blocks(mixed.at[t], inbox.at[t], fs.at[t], fr.at[t])

    make_forcing(2)

    pltpu.make_async_copy(rates.at[pl.ds(g * 8, 16)], rates_in.at[0, pl.ds(lon * 16, 16)], rr.at[0]).start()

    def send_rates(k, carry):
        target = lax.rem(lon + k, N_LON)
        to = group_of_lon(target)
        src = rates.at[pl.ds(to * 8, 16)]

        @pl.when(k > 0)
        def _():
            remote(src, rates_in.at[0, pl.ds(lon * 16, 16)], rs.at[0], rr.at[0], target, lat).start()

        remote(src, rates_in.at[1, pl.ds(lon * 16, 16)], rs.at[1], rr.at[1], target, south).start()
        remote(src, rates_in.at[2, pl.ds(lon * 16, 16)], rs.at[2], rr.at[2], target, north).start()
        return carry

    lax.fori_loop(0, N_LON, send_rates, 0)
    for t in range(3):
        convert_courant(t)
    pltpu.make_async_copy(
        courant_out.at[pl.ds(0, 3), pl.ds(g * 32, 32)], courant_in.at[pl.ds(0, 3), pl.ds(lon * 32, 32)], kr.at[0]
    ).start()

    def send_courant(to, target):
        remote(
            courant_out.at[pl.ds(0, 3), pl.ds(to * 32, 32)],
            courant_in.at[pl.ds(0, 3), pl.ds(lon * 32, 32)],
            ks.at[0], kr.at[0], target, lat,
        ).start()

    to_groups(send_courant)
    send_tiles(1, False)

    lane = lax.broadcasted_iota(jnp.int32, (16, 128), 1)
    flux[...] = jnp.zeros_like(flux)

    def loop_block(ref, at, first, stride):
        half = 8 * stride
        return jnp.concatenate(
            [ref[at, pl.ds(first, 8, stride=stride)], ref[at, pl.ds(first + half, 8, stride=stride)]], axis=0
        )

    def put_twice(i, value):
        twice[i, pl.ds(0, 16)] = value
        twice[i, pl.ds(16, 16)] = value

    def roll_rows(t):
        for row in range(6):
            i, j = (0, 3) if row == 0 else (2, 0) if row == 5 else (1, row - 1)
            shift = shifts[i, SHIFT_LANE + t * 4 + j]
            q, r = shift // 128, lax.rem(shift, 128)
            back = lax.rem(128 - r, 128)
            inside = lane < 128 - r

            def body(n, carry, row=row, q=q, back=back, inside=inside):
                i = row * 8 + n
                first = pltpu.roll(twice[i, pl.ds(q, 16)], back, 1)
                second = pltpu.roll(twice[i, pl.ds(q + 1, 16)], back, 1)
                value = jnp.where(inside, first, second)
                if row == 0:
                    value = jnp.where(lat == 0, 0.0, value)
                if row == 5:
                    value = jnp.where(lat == N_LAT - 1, 0.0, value)
                rolled[i] = value
                return carry

            lax.fori_loop(0, 8, body, 0, unroll=True)

    def transport(t, finish):
        def body(n, carry):
            l, row = n // 4, lax.rem(n, 4)
            faces = [
                jnp.concatenate(
                    [
                        courant_in[t, pl.ds(face * 8 + n, 8, stride=32)],
                        courant_in[t, pl.ds(256 + face * 8 + n, 8, stride=32)],
                    ],
                    axis=0,
                )
                for face in range(4)
            ]
            for c in range(4):
                i = (row + 1) * 8 + l * 4 + c
                x, up, down = rolled[i], rolled[i + 8], rolled[i - 8]
                e = pltpu.roll(x, 127, 1)
                east = jnp.where(lane == 127, pltpu.roll(e, 15, 0), e)
                w = pltpu.roll(x, 1, 1)
                west = jnp.where(lane == 0, pltpu.roll(w, 1, 0), w)
                value = (
                    x + faces[0] * (up - x) + faces[1] * (down - x) + faces[2] * (east - x) + faces[3] * (west - x)
                )
                finish(c, l, row, n, value)
            return carry

        lax.fori_loop(0, 8, body, 0, unroll=True)
        return None

    def add_forcing(t, e):
        def finish(c, l, row, n, value):
            at = pl.ds((c * 4 + row) * 16, 16)

            @pl.when(l == 0)
            def _():
                flux[at] = flux[at] + value

            state[e, row + 1, l + 1, c] = value + loop_block(inbox, t, c * 8 + n, 32)

        return finish

    def exchange(e):
        return [
            remote(state.at[e, pl.ds(1, 4), 2], state.at[e, pl.ds(1, 4), 0], es.at[e, 0], er.at[e, 0], lon_up, lat),
            remote(state.at[e, pl.ds(1, 4), 1], state.at[e, pl.ds(1, 4), 3], es.at[e, 1], er.at[e, 1], lon_down, lat),
            remote(state.at[e, 1, pl.ds(1, 2)], state.at[e, 5, pl.ds(1, 2)], es.at[e, 2], er.at[e, 2], lon, north),
            remote(state.at[e, 4, pl.ds(1, 2)], state.at[e, 0, pl.ds(1, 2)], es.at[e, 3], er.at[e, 3], lon, south),
            remote(state.at[e, 1, 2], state.at[e, 5, 0], es.at[e, 4], er.at[e, 4], lon_up, north),
            remote(state.at[e, 4, 2], state.at[e, 0, 0], es.at[e, 5], er.at[e, 5], lon_up, south),
            remote(state.at[e, 1, 1], state.at[e, 5, 3], es.at[e, 6], er.at[e, 6], lon_down, north),
            remote(state.at[e, 4, 1], state.at[e, 0, 3], es.at[e, 7], er.at[e, 7], lon_down, south),
        ]

    def mix_rows(e):
        for row in range(6):
            for l in range(2):
                low, high = rates_t[row, l], rates_t[row, l + 1]

                def body(c, carry, row=row, l=l, low=low, high=high):
                    mid = state[e, row, l + 1, c]
                    value = mid + high * (state[e, row, l + 2, c] - mid) - low * (mid - state[e, row, l, c])
                    put_twice(row * 8 + l * 4 + c, value)
                    return carry

                lax.fori_loop(0, 4, body, 0, unroll=True)

    wait_bytes(inbox.at[3], pr.at[0])
    wait_bytes(halo.at[0], pr.at[1])
    wait_bytes(halo.at[1], pr.at[2])
    for i in range(3):
        wait_bytes(note_in.at[pl.ds(0, 1)], sm.at[i])
    for l in range(2):
        for c in range(4):
            put_twice(l * 4 + c, loop_block(halo, 0, l * 4 + c, 8))
            put_twice(40 + l * 4 + c, loop_block(halo, 1, l * 4 + c, 8))
            for row in range(4):
                put_twice((row + 1) * 8 + l * 4 + c, loop_block(inbox, 3, c * 8 + l * 4 + row, 32))
    roll_rows(3)
    wait_bytes(courant_in.at[3], kr.at[1])
    wait_bytes(inbox.at[2], fr.at[2])
    transport(3, add_forcing(2, 0))
    moves = exchange(0)
    for move in moves:
        move.start()

    send_tiles(0, False)
    make_forcing(1)
    for i in range(3):
        wait_bytes(rates_in.at[i], rr.at[i])
    for level in range(3):
        for row in range(6):
            i, j = (1, 3) if row == 0 else (2, 0) if row == 5 else (0, row - 1)
            rates_t[row, level] = loop_block(rates_in, i, (level + 1) * 4 + j, 16)
    wait_bytes(courant_in.at[pl.ds(0, 3)], kr.at[0])

    for t in (2, 1):
        for move in moves:
            move.wait_recv()
        mix_rows(2 - t)
        roll_rows(t)
        wait_bytes(inbox.at[t - 1], fr.at[t - 1])
        transport(t, add_forcing(t - 1, 3 - t))
        for move in moves:
            move.wait_send()
        moves = exchange(3 - t)
        for move in moves:
            move.start()
        if t == 2:
            make_forcing(0)

    for move in moves:
        move.wait_recv()
    mix_rows(2)
    roll_rows(0)

    def finish(c, l, row, n, value):
        at = pl.ds((c * 4 + row) * 16, 16)

        @pl.when(l == 0)
        def _():
            flux[at] = flux[at] + value

        final[pl.ds((c * 8 + n) * 16, 16)] = value

    transport(0, finish)

    for d in range(N_LON):
        for c in range(4):
            final_out[d, c] = final[pl.ds(c * 128 + d, 8, stride=16)]
        flux_send[d] = flux[pl.ds(d, 16, stride=16)]
    mine = out.at[:, pl.ds(g * 8, 8)]
    pltpu.make_async_copy(final_out.at[lon], mine, orv).start()

    def send_out(k, carry):
        target = lax.rem(lon + k, N_LON)
        remote(final_out.at[target], mine, os, orv, target, lat).start()
        return carry

    lax.fori_loop(1, N_LON, send_out, 0)

    @pl.when(g == 0)
    def _():
        pltpu.make_async_copy(flux_send.at[lon], flux_out, xr).start()

        def send_flux(k, carry):
            target = lax.rem(lon + k, N_LON)
            remote(flux_send.at[target], flux_out, xs, xr, target, lat).start()
            return carry

        lax.fori_loop(1, N_LON, send_flux, 0)
        wait_bytes(flux_send.at[pl.ds(0, N_LON - 1)], xs)

    for move in moves:
        move.wait_send()
    for t in range(4):
        wait_bytes(jac_in.at[t, pl.ds(0, 8 * (N_DEV - 1))], js.at[t])
    wait_bytes(note_in.at[pl.ds(0, N_DEV - 1)], ns)
    wait_bytes(inbox.at[3, pl.ds(0, 480)], ps.at[0])
    wait_bytes(halo.at[0], ps.at[1])
    wait_bytes(halo.at[1], ps.at[2])
    for t in range(3):
        wait_bytes(inbox.at[t, pl.ds(0, 480)], fs.at[t])
    wait_bytes(courant_in.at[3, pl.ds(0, 480)], ks.at[1])
    wait_bytes(courant_in.at[pl.ds(0, 3), pl.ds(0, 480)], ks.at[0])
    wait_bytes(rates_in.at[0, pl.ds(0, 240)], rs.at[0])
    wait_bytes(rates_in.at[1], rs.at[1])
    wait_bytes(rates_in.at[2], rs.at[2])
    wait_bytes(final_out.at[pl.ds(0, N_LON - 1)], os)
    wait_bytes(out, orv)
    wait_bytes(flux_out, xr)


def shards(adjoint_end, face_courant, mixing, row_shift, tile_jac, tile_cell, tile_count):
    slots = lax.broadcasted_iota(jnp.int32, (4, N_DEV, 8), 2)
    cells = jnp.where(slots < tile_count[0][:, :, None], tile_cell[0], -1)
    cells = jnp.transpose(cells, (1, 0, 2)).reshape(N_DEV, 32)
    own_shift = jnp.broadcast_to(row_shift.reshape(1, 16), (N_DEV, 16))
    note = jnp.concatenate([cells, own_shift, jnp.zeros((N_DEV, 80), jnp.int32)], axis=1)
    dma = pltpu.SemaphoreType.DMA
    vmem = pltpu.VMEM
    whole = pl.BlockSpec(memory_space=pltpu.VMEM)
    out, flux = pl.pallas_call(
        kernel,
        out_shape=(
            jax.ShapeDtypeStruct((4, 128, 128), F32),
            jax.ShapeDtypeStruct((16, 128), F32),
        ),
        in_specs=[whole, whole, whole, pl.BlockSpec(memory_space=pl.ANY), whole],
        out_specs=(whole, whole),
        scratch_shapes=[
            vmem((4, 1024, 128), F32),
            vmem((128, 128), jnp.int32),
            pltpu.SMEM((3, 128), jnp.int32),
            vmem((4, 128, 128), F32),
            vmem((4, 144, 128), F32),
            vmem((144, 128), F32),
            vmem((4, 512, 128), F32),
            vmem((2, 128, 128), F32),
            vmem((4, 512, 128), F32),
            vmem((4, 512, 128), F32),
            vmem((2, 128, 128), F32),
            vmem((4, 512, 128), F32),
            vmem((3, 256, 128), F32),
            vmem((6, 3, 16, 128), F32),
            vmem((3, 6, 4, 4, 16, 128), F32),
            vmem((48, 32, 128), F32),
            vmem((48, 16, 128), F32),
            vmem((512, 128), F32),
            vmem((16, 4, 8, 128), F32),
            vmem((256, 128), F32),
            vmem((16, 16, 128), F32),
            dma((4,)), dma((4,)), dma, dma, dma((3,)), dma((3,)), dma((3,)), dma((3,)), dma((2,)), dma((2,)),
            dma((3,)), dma((3,)), dma((3, 8)), dma((3, 8)), dma, dma, dma, dma, dma((3,)),
        ],
        compiler_params=pltpu.CompilerParams(
            collective_id=0, has_side_effects=True, vmem_limit_bytes=48 * 1024 * 1024
        ),
    )(
        adjoint_end.reshape(4, 128, 128),
        face_courant,
        mixing,
        tile_jac.reshape(4, 1024, 128),
        note,
    )
    return out.reshape(4, 32, 4, 128), flux.reshape(4, 4, 128)


def solution(mesh):
    in_specs = (
        P(None, None, "lat", "lon"),
        P(None, None, None, "lat", "lon"),
        P(None, "lat", "lon"),
        P(None, "lat"),
        P(("lon", "lat"), None, None, None, None),
        P(("lon", "lat"), None, None, None),
        P(("lon", "lat"), None, None),
    )
    out_specs = (P(None, None, "lat", "lon"), P(None, "lat", "lon"))
    return jax.shard_map(shards, mesh=mesh, in_specs=in_specs, out_specs=out_specs, check_vma=False)
```

```python
import functools

import jax
import jax.numpy as jnp
from jax import lax
from jax.experimental import pallas as pl
from jax.experimental.pallas import tpu as pltpu
from jax.sharding import PartitionSpec as P

MESH = pl.DeviceIdType.MESH
F32 = jnp.float32
N_LON = 16
N_LAT = 8
N_DEV = N_LON * N_LAT
SHIFT_LANE = 32
ORDER = {
    "wait3": ("courant3", "send_cells", "turn2", "tiles2", "turn1", "send_rates", ),
    "sent1": ("tiles1", "courant2", "courant1", "pass_rates", ),
    "rolled3": ("wait_cells", "scatter2", ),
    "sentE2": ("turn0", "tiles0", "courant0", "scatter1", "wait_rates", ),
    "rolled2": (),
    "sentE1": ("scatter0", ),
    "rolled1": (),
    "sentE0": (),
}


def lon_of_group(g):
    k = g // 2
    x_hi = k // 4
    z = k + x_hi * (7 - 2 * k)
    return z * 4 + x_hi * 2 + g % 2


def group_of_lon(lon):
    z = lon // 4
    k = z + (lon // 2) % 2 * (7 - 2 * z)
    return k * 2 + lon % 2


def remote(src, dst, send_sem, recv_sem, lon, lat):
    return pltpu.make_async_remote_copy(
        src_ref=src,
        dst_ref=dst,
        send_sem=send_sem,
        recv_sem=recv_sem,
        device_id=(lon, lat),
        device_id_type=MESH,
    )


def wait_bytes(ref, sem):
    pltpu.make_async_copy(ref, ref, sem).wait()


def kernel(
    adj_hbm, courant_hbm, mixing_hbm, shift_hbm, jac, cell_hbm, count_hbm,
    out, flux_out,
    adj, courant, mixing, own_shift, cell, count, note, raw, tiles_out, cells_out, cells_in, cells_t, values_t, force,
    jac_in, note_in, shifts, forcing, padded, rates, mixed, edges, courant_out,
    inbox, halo, courant_in, rates_in, rates_t, state, twice, rolled, final, final_out, flux, flux_send,
    js, jr, ns, nr, ps, pr, ks, kr, rs, rr, es, er, os, orv, xs, xr, sm, ls, ws, wr, cs, cr, ts,
):
    lon, lat = lax.axis_index("lon"), lax.axis_index("lat")
    me = lon * N_LAT + lat
    g = group_of_lon(lon)
    north, south = lax.rem(lat + N_LAT - 1, N_LAT), lax.rem(lat + 1, N_LAT)
    lon_up, lon_down = lon_of_group(lax.rem(g + 1, N_LON)), lon_of_group(lax.rem(g + N_LON - 1, N_LON))

    loads = [
        pltpu.make_async_copy(src, dst, ls.at[i])
        for i, (src, dst) in enumerate(
            (
                (cell_hbm, cell), (count_hbm, count), (shift_hbm, own_shift),
                (courant_hbm, courant), (mixing_hbm, mixing), (adj_hbm, adj),
            )
        )
    ]
    for load in loads:
        load.start()
    for t in (2, 1, 0):
        pltpu.make_async_copy(jac.at[t], raw.at[t], ts.at[t]).start()

    barrier = pltpu.get_barrier_semaphore()

    def peer(k):
        return lax.rem(lon + k // N_LAT, N_LON), lax.rem(lat + k % N_LAT, N_LAT)

    def greet(k, carry):
        pl.semaphore_signal(barrier, inc=1, device_id=peer(k), device_id_type=MESH)
        return carry

    lax.fori_loop(1, N_DEV, greet, 0)

    for load in loads[:3]:
        load.wait()
    slots = lax.broadcasted_iota(jnp.int32, (8, 128), 0)
    lines = [jnp.where(slots < count[t : t + 1], cell[t], -1) for t in range(4)]
    lines += [jnp.full((1, 128), own_shift[i // 4, i % 4], jnp.int32) for i in range(16)]
    by_owner = jnp.transpose(jnp.concatenate(lines + [jnp.zeros((80, 128), jnp.int32)], axis=0))
    note[...] = by_owner

    owner_lane = lax.broadcasted_iota(jnp.int32, (8, 128), 1) // 8
    for t in range(3):
        line = jnp.zeros((8, 128), jnp.int32)
        for d in range(N_LON):
            turned = pltpu.roll(by_owner[d * 8 : d * 8 + 8], (d * 8 - t * 8) % 128, 1)
            line = jnp.where(owner_lane == d, turned, line)
        cells_out[t] = line

    pl.semaphore_wait(barrier, N_DEV - 1)

    def send_tiles(t, notes):
        def body(k, carry):
            p_lon, p_lat = peer(k)
            owner = p_lon * N_LAT + p_lat
            if notes:
                remote(note.at[pl.ds(owner, 1)], note_in.at[pl.ds(me, 1)], ns, nr, p_lon, p_lat).start()
            remote(
                jac.at[t, pl.ds(owner * 8, 8)], jac_in.at[t, pl.ds(me * 8, 8)], js.at[t], jr.at[t], p_lon, p_lat
            ).start()
            return carry

        if notes:
            pltpu.make_async_copy(note.at[pl.ds(me, 1)], note_in.at[pl.ds(me, 1)], nr).start()
        pltpu.make_async_copy(jac.at[t, pl.ds(me * 8, 8)], jac_in.at[t, pl.ds(me * 8, 8)], jr.at[t]).start()
        lax.fori_loop(1, N_DEV, body, 0)

    def turn_tiles(t):
        pltpu.make_async_copy(jac.at[t], raw.at[t], ts.at[t]).wait()

        def body(p, carry):
            rows = [raw[t, pl.ds((d * N_LAT + p) * 8, 8)] for d in range(N_LON)]
            entries = jnp.transpose(jnp.concatenate(rows, axis=0))
            for c in range(4):
                tiles_out[t, p, pl.ds(c, 32, stride=4)] = entries[c * 32 : c * 32 + 32]
            return carry

        lax.fori_loop(0, N_LAT, body, 0)

    def send_turned(t):
        def body(k, carry):
            p_lon, p_lat = peer(k)
            remote(
                tiles_out.at[t, p_lat, pl.ds(group_of_lon(p_lon) * 8, 8)],
                jac_in.at[t, pl.ds(me * 8, 8)],
                js.at[t], jr.at[t], p_lon, p_lat,
            ).start()
            return carry

        pltpu.make_async_copy(
            tiles_out.at[t, lat, pl.ds(g * 8, 8)], jac_in.at[t, pl.ds(me * 8, 8)], jr.at[t]
        ).start()
        lax.fori_loop(1, N_DEV, body, 0)

    def send_cells():
        def body(k, carry):
            p_lon, p_lat = peer(k)
            remote(
                cells_out.at[:, pl.ds(p_lat, 1)], cells_in.at[:, pl.ds(me, 1)], cs, cr, p_lon, p_lat
            ).start()
            return carry

        pltpu.make_async_copy(cells_out.at[:, pl.ds(lat, 1)], cells_in.at[:, pl.ds(me, 1)], cr).start()
        lax.fori_loop(1, N_DEV, body, 0)

    def scatter_loop(t):
        wait_bytes(jac_in.at[t], jr.at[t])
        cells_t[...] = jnp.transpose(cells_in[t])
        for e in range(8):
            values_t[pl.ds(e * 128, 128)] = jnp.transpose(jac_in[t, pl.ds(e, 128, stride=8)])
        columns = lax.broadcasted_iota(jnp.int32, (128, 128), 0)

        def body(d, carry):
            left, right = [], []
            for slot in range(8):
                place = cells_t[pl.ds(d * 8 + slot, 1)]
                row, column = place >> 7, place & 127
                value = values_t[pl.ds(d * 8 + slot, 8, stride=128)]
                value = jnp.concatenate([jnp.where(row == r, value, 0.0) for r in range(4)], axis=0)
                high = value.astype(jnp.bfloat16)
                low = (value - high.astype(F32)).astype(jnp.bfloat16)
                left.append(jnp.concatenate([high, low], axis=0))
                right.append(jnp.where(columns == column, 1.0, 0.0).astype(jnp.bfloat16))
            total = lax.dot_general(
                jnp.concatenate(left, axis=1),
                jnp.concatenate(right, axis=1),
                (((1,), (1,)), ((), ())),
                preferred_element_type=F32,
            )
            force[t, pl.ds(d, 32, stride=16)] = total[:32] + total[32:]
            return carry

        lax.fori_loop(0, N_LON, body, 0)

    def to_groups(send):
        def body(k, carry):
            target = lax.rem(lon + k, N_LON)
            send(group_of_lon(target), target)
            return carry

        lax.fori_loop(1, N_LON, body, 0)

    def send_blocks(src, dst, send_sem, recv_sem):
        pltpu.make_async_copy(src.at[pl.ds(g * 32, 32)], dst.at[pl.ds(lon * 32, 32)], recv_sem).start()

        def one(to, target):
            remote(
                src.at[pl.ds(to * 32, 32)], dst.at[pl.ds(lon * 32, 32)], send_sem, recv_sem, target, lat
            ).start()

        to_groups(one)

    def convert_courant(t):
        for face in range(4):
            values = courant[face, t].astype(F32).reshape(128, 128)
            for to in range(N_LON):
                courant_out[t, pl.ds(to * 32 + face * 8, 8)] = values[to * 8 : to * 8 + 8]

    def scatter(t):
        cells = jnp.transpose(note_in[...].astype(F32))
        cell_ids = lax.broadcasted_iota(jnp.int32, (512, 128), 0).astype(F32)
        total = jnp.zeros((512, 256), F32)
        for pair in range(4):
            hot, value = [], []
            for slot in (2 * pair, 2 * pair + 1):
                row = cells[t * 8 + slot : t * 8 + slot + 1]
                hot.append(jnp.where(cell_ids == row, 1.0, 0.0).astype(jnp.bfloat16))
                x = jac_in[t, pl.ds(slot, 128, stride=8)]
                high = x.astype(jnp.bfloat16)
                low = (x - high.astype(F32)).astype(jnp.bfloat16)
                value.append(jnp.concatenate([high, low], axis=1))
            total = total + jnp.dot(
                jnp.concatenate(hot, axis=1), jnp.concatenate(value, axis=0), preferred_element_type=F32
            )
        both = total[:, :128] + total[:, 128:]
        for row in range(4):
            by_entry = jnp.transpose(both[row * 128 : row * 128 + 128])
            for c in range(4):
                forcing[c, pl.ds(row, 32, stride=4)] = by_entry[c * 32 : c * 32 + 32]

    def send_rates():
        loads[4].wait()
        rates[...] = jnp.zeros_like(rates)
        rates[pl.ds(8, 124)] = mixing[...].astype(F32).reshape(124, 128)
        pltpu.make_async_copy(rates.at[pl.ds(8 + g * 8, 8)], rates_in.at[pl.ds(lon * 8, 8)], rr.at[0]).start()

        def one(to, target):
            remote(
                rates.at[pl.ds(8 + to * 8, 8)], rates_in.at[pl.ds(lon * 8, 8)], rs.at[0], rr.at[0], target, lat
            ).start()

        to_groups(one)

    rate_moves = [
        remote(rates_t.at[pl.ds(1, 4), 2], rates_t.at[pl.ds(1, 4), 0], ws.at[0], wr.at[0], lon_up, lat),
        remote(rates_t.at[1, pl.ds(1, 2)], rates_t.at[5, pl.ds(1, 2)], ws.at[1], wr.at[1], lon, north),
        remote(rates_t.at[4, pl.ds(1, 2)], rates_t.at[0, pl.ds(1, 2)], ws.at[2], wr.at[2], lon, south),
        remote(rates_t.at[1, 2], rates_t.at[5, 0], ws.at[3], wr.at[3], lon_up, north),
        remote(rates_t.at[4, 2], rates_t.at[0, 0], ws.at[4], wr.at[4], lon_up, south),
    ]

    def pass_rates():
        wait_bytes(rates_in, rr.at[0])
        for l in range(2):
            for row in range(4):
                n = l * 4 + row
                rates_t[row + 1, l + 1] = jnp.concatenate(
                    [rates_in[pl.ds(n, 8, stride=8)], rates_in[pl.ds(64 + n, 8, stride=8)]], axis=0
                )
        for move in rate_moves:
            move.start()

    def wait_rates():
        for move in rate_moves:
            move.wait_recv()

    def do(slot):
        for name in ORDER[slot]:
            what, t = name[:-1], int(name[-1]) if name[-1].isdigit() else None
            if what == "courant":
                convert_courant(t)
                send_blocks(courant_out.at[t], courant_in.at[t], ks.at[t], kr.at[t])
            elif what == "turn":
                turn_tiles(t)
            elif what == "tiles":
                send_turned(t)
            elif what == "scatter":
                scatter_loop(t)
            else:
                {"send_rates": send_rates, "pass_rates": pass_rates, "wait_rates": wait_rates,
                 "send_cells": send_cells, "wait_cells": lambda: wait_bytes(cells_in, cr)}[name]()

    send_tiles(3, True)
    loads[3].wait()
    do("wait3")
    wait_bytes(note_in, nr)
    for i, row in enumerate((north, lat, south)):
        pltpu.make_async_copy(note_in.at[pl.ds(lon * N_LAT + row, 1)], shifts.at[pl.ds(i, 1)], sm.at[i]).start()
    wait_bytes(jac_in.at[3], jr.at[3])
    scatter(3)

    loads[5].wait()
    padded[...] = jnp.zeros_like(padded)
    for c in range(4):
        padded[c, pl.ds(8, 128)] = adj[c] + forcing[c]
        mid, above, below = padded[c, pl.ds(8, 128)], padded[c, pl.ds(12, 128)], padded[c, pl.ds(4, 128)]
        value = mid + rates[pl.ds(8, 128)] * (above - mid) - rates[pl.ds(4, 128)] * (mid - below)
        for to in range(N_LON):
            mixed[0, pl.ds(to * 32 + c * 8, 8)] = value[to * 8 : to * 8 + 8]
        padded[c, pl.ds(8, 128)] = value
        edges[0, pl.ds(c, 32, stride=4)] = padded[c, pl.ds(8, 32, stride=4)]
        edges[1, pl.ds(c, 32, stride=4)] = padded[c, pl.ds(11, 32, stride=4)]
    send_blocks(mixed.at[0], inbox.at[0], ps.at[0], pr.at[0])

    def send_edges(k, carry):
        target = lax.rem(lon + k, N_LON)
        to = group_of_lon(target)
        remote(
            edges.at[1, pl.ds(to * 8, 8)], halo.at[0, pl.ds(lon * 8, 8)], ps.at[1], pr.at[1], target, south
        ).start()
        remote(
            edges.at[0, pl.ds(to * 8, 8)], halo.at[1, pl.ds(lon * 8, 8)], ps.at[2], pr.at[2], target, north
        ).start()
        return carry

    lax.fori_loop(0, N_LON, send_edges, 0)

    do("sent1")

    lane = lax.broadcasted_iota(jnp.int32, (16, 128), 1)
    flux[...] = jnp.zeros_like(flux)

    def loop_block(ref, at, first, stride):
        half = 8 * stride
        return jnp.concatenate(
            [ref[at, pl.ds(first, 8, stride=stride)], ref[at, pl.ds(first + half, 8, stride=stride)]], axis=0
        )

    def put_twice(i, value):
        twice[i, pl.ds(0, 16)] = value
        twice[i, pl.ds(16, 16)] = value

    def roll_rows(t):
        for row in range(6):
            i, j = (0, 3) if row == 0 else (2, 0) if row == 5 else (1, row - 1)
            shift = shifts[i, SHIFT_LANE + t * 4 + j]
            q, r = shift // 128, lax.rem(shift, 128)
            back = lax.rem(128 - r, 128)
            inside = lane < 128 - r

            def body(n, carry, row=row, q=q, back=back, inside=inside):
                i = row * 8 + n
                first = pltpu.roll(twice[i, pl.ds(q, 16)], back, 1)
                second = pltpu.roll(twice[i, pl.ds(q + 1, 16)], back, 1)
                value = jnp.where(inside, first, second)
                if row == 0:
                    value = jnp.where(lat == 0, 0.0, value)
                if row == 5:
                    value = jnp.where(lat == N_LAT - 1, 0.0, value)
                rolled[i] = value
                return carry

            lax.fori_loop(0, 8, body, 0, unroll=True)

    def transport(t, finish):
        def body(n, carry):
            l, row = n // 4, lax.rem(n, 4)
            faces = [
                jnp.concatenate(
                    [
                        courant_in[t, pl.ds(face * 8 + n, 8, stride=32)],
                        courant_in[t, pl.ds(256 + face * 8 + n, 8, stride=32)],
                    ],
                    axis=0,
                )
                for face in range(4)
            ]
            for c in range(4):
                i = (row + 1) * 8 + l * 4 + c
                x, up, down = rolled[i], rolled[i + 8], rolled[i - 8]
                e = pltpu.roll(x, 127, 1)
                east = jnp.where(lane == 127, pltpu.roll(e, 15, 0), e)
                w = pltpu.roll(x, 1, 1)
                west = jnp.where(lane == 0, pltpu.roll(w, 1, 0), w)
                value = (
                    x + faces[0] * (up - x) + faces[1] * (down - x) + faces[2] * (east - x) + faces[3] * (west - x)
                )
                finish(c, l, row, n, value)
            return carry

        lax.fori_loop(0, 8, body, 0, unroll=True)
        return None

    def add_forcing(t, e):
        def finish(c, l, row, n, value):
            at = pl.ds((c * 4 + row) * 16, 16)

            @pl.when(l == 0)
            def _():
                flux[at] = flux[at] + value

            state[e, row + 1, l + 1, c] = value + force[t, pl.ds(((row * 2 + l) * 4 + c) * 16, 16)]

        return finish

    def exchange(e):
        own, first, last = pl.ds(1, 4), 1, 4
        moves = []
        for dg, dl in ((1, 0), (-1, 0), (0, -1), (0, 1), (1, -1), (1, 1), (-1, -1), (-1, 1)):
            rows = own if dl == 0 else first if dl < 0 else last
            to_rows = own if dl == 0 else 5 if dl < 0 else 0
            levels = pl.ds(1, 2) if dg == 0 else 2 if dg > 0 else 1
            to_levels = pl.ds(1, 2) if dg == 0 else 0 if dg > 0 else 3
            i = len(moves)
            move = remote(
                state.at[e, rows, levels], state.at[e, to_rows, to_levels], es.at[e, i], er.at[e, i],
                lon if dg == 0 else lon_up if dg > 0 else lon_down,
                lat if dl == 0 else north if dl < 0 else south,
            )
            sends, gets = [], []
            if dg:
                sends.append(g < N_LON - 1 if dg > 0 else g > 0)
                gets.append(g > 0 if dg > 0 else g < N_LON - 1)
            if dl:
                sends.append(lat > 0 if dl < 0 else lat < N_LAT - 1)
                gets.append(lat < N_LAT - 1 if dl < 0 else lat > 0)
            moves.append((move, functools.reduce(jnp.logical_and, sends), functools.reduce(jnp.logical_and, gets)))
        return moves

    def start_moves(moves):
        for move, sends, _ in moves:
            pl.when(sends)(move.start)

    def wait_moves(moves):
        for move, _, gets in moves:
            pl.when(gets)(move.wait_recv)

    def end_moves(moves):
        for move, sends, _ in moves:
            pl.when(sends)(move.wait_send)

    @pl.when(g == 0)
    def _():
        for e in range(3):
            state[e, :, 0] = jnp.zeros_like(state[e, :, 0])

    @pl.when(g == N_LON - 1)
    def _():
        for e in range(3):
            state[e, :, 3] = jnp.zeros_like(state[e, :, 3])

    def mix_rows(e):
        for row in range(6):
            for l in range(2):
                low, high = rates_t[row, l], rates_t[row, l + 1]

                def body(c, carry, row=row, l=l, low=low, high=high):
                    mid = state[e, row, l + 1, c]
                    value = mid + high * (state[e, row, l + 2, c] - mid) - low * (mid - state[e, row, l, c])
                    put_twice(row * 8 + l * 4 + c, value)
                    return carry

                lax.fori_loop(0, 4, body, 0, unroll=True)

    wait_bytes(inbox.at[0], pr.at[0])
    wait_bytes(halo.at[0], pr.at[1])
    wait_bytes(halo.at[1], pr.at[2])
    for i in range(3):
        wait_bytes(note_in.at[pl.ds(0, 1)], sm.at[i])
    for l in range(2):
        for c in range(4):
            put_twice(l * 4 + c, loop_block(halo, 0, l * 4 + c, 8))
            put_twice(40 + l * 4 + c, loop_block(halo, 1, l * 4 + c, 8))
            for row in range(4):
                put_twice((row + 1) * 8 + l * 4 + c, loop_block(inbox, 0, c * 8 + l * 4 + row, 32))
    roll_rows(3)
    wait_bytes(courant_in.at[3], kr.at[3])
    do("rolled3")
    transport(3, add_forcing(2, 0))
    moves = exchange(0)
    start_moves(moves)

    do("sentE2")

    for t in (2, 1):
        wait_moves(moves)
        mix_rows(2 - t)
        roll_rows(t)
        wait_bytes(courant_in.at[t], kr.at[t])
        do(f"rolled{t}")
        transport(t, add_forcing(t - 1, 3 - t))
        end_moves(moves)
        moves = exchange(3 - t)
        start_moves(moves)
        do(f"sentE{t - 1}")

    wait_moves(moves)
    mix_rows(2)
    roll_rows(0)
    wait_bytes(courant_in.at[0], kr.at[0])

    def finish(c, l, row, n, value):
        at = pl.ds((c * 4 + row) * 16, 16)

        @pl.when(l == 0)
        def _():
            flux[at] = flux[at] + value

        final[pl.ds((c * 8 + n) * 16, 16)] = value

    transport(0, finish)

    for d in range(N_LON):
        for c in range(4):
            final_out[d, c] = final[pl.ds(c * 128 + d, 8, stride=16)]
        flux_send[d] = flux[pl.ds(d, 16, stride=16)]
    mine = out.at[:, pl.ds(g * 8, 8)]
    pltpu.make_async_copy(final_out.at[lon], mine, orv).start()

    def send_out(k, carry):
        target = lax.rem(lon + k, N_LON)
        remote(final_out.at[target], mine, os, orv, target, lat).start()
        return carry

    lax.fori_loop(1, N_LON, send_out, 0)

    @pl.when(g == 0)
    def _():
        pltpu.make_async_copy(flux_send.at[lon], flux_out, xr).start()

        def send_flux(k, carry):
            target = lax.rem(lon + k, N_LON)
            remote(flux_send.at[target], flux_out, xs, xr, target, lat).start()
            return carry

        lax.fori_loop(1, N_LON, send_flux, 0)
        wait_bytes(flux_send.at[pl.ds(0, N_LON - 1)], xs)

    end_moves(moves)
    for t in range(4):
        wait_bytes(jac_in.at[t, pl.ds(0, 8 * (N_DEV - 1))], js.at[t])
    wait_bytes(note_in.at[pl.ds(0, N_DEV - 1)], ns)
    wait_bytes(cells_in.at[:, pl.ds(0, N_DEV - 1)], cs)
    wait_bytes(inbox.at[0, pl.ds(0, 480)], ps.at[0])
    wait_bytes(halo.at[0], ps.at[1])
    wait_bytes(halo.at[1], ps.at[2])
    for t in range(4):
        wait_bytes(courant_in.at[t, pl.ds(0, 480)], ks.at[t])
    wait_bytes(rates_in.at[pl.ds(0, 120)], rs.at[0])
    for move in rate_moves:
        move.wait_send()
    wait_bytes(final_out.at[pl.ds(0, N_LON - 1)], os)
    wait_bytes(out, orv)
    wait_bytes(flux_out, xr)


def shards(adjoint_end, face_courant, mixing, row_shift, tile_jac, tile_cell, tile_count):
    dma = pltpu.SemaphoreType.DMA
    vmem = pltpu.VMEM
    whole = pl.BlockSpec(memory_space=pltpu.VMEM)
    out, flux = pl.pallas_call(
        kernel,
        out_shape=(
            jax.ShapeDtypeStruct((4, 128, 128), F32),
            jax.ShapeDtypeStruct((16, 128), F32),
        ),
        in_specs=[pl.BlockSpec(memory_space=pl.ANY)] * 7,
        out_specs=(whole, whole),
        scratch_shapes=[
            vmem((4, 128, 128), F32),
            vmem((4, 4, 32, 4, 128), jnp.bfloat16),
            vmem((31, 4, 128), jnp.bfloat16),
            pltpu.SMEM((4, 4), jnp.int32),
            vmem((4, 8, 128), jnp.int32),
            vmem((4, 128), jnp.int32),
            vmem((128, 128), jnp.int32),
            vmem((3, 1024, 128), F32),
            vmem((3, 8, 128, 128), F32),
            vmem((3, 8, 128), jnp.int32),
            vmem((3, 128, 128), jnp.int32),
            vmem((128, 128), jnp.int32),
            vmem((1024, 128), F32),
            vmem((3, 512, 128), F32),
            vmem((4, 1024, 128), F32),
            vmem((128, 128), jnp.int32),
            pltpu.SMEM((3, 128), jnp.int32),
            vmem((4, 128, 128), F32),
            vmem((4, 144, 128), F32),
            vmem((144, 128), F32),
            vmem((1, 512, 128), F32),
            vmem((2, 128, 128), F32),
            vmem((4, 512, 128), F32),
            vmem((1, 512, 128), F32),
            vmem((2, 128, 128), F32),
            vmem((4, 512, 128), F32),
            vmem((128, 128), F32),
            vmem((6, 3, 16, 128), F32),
            vmem((3, 6, 4, 4, 16, 128), F32),
            vmem((48, 32, 128), F32),
            vmem((48, 16, 128), F32),
            vmem((512, 128), F32),
            vmem((16, 4, 8, 128), F32),
            vmem((256, 128), F32),
            vmem((16, 16, 128), F32),
            dma((4,)), dma((4,)), dma, dma, dma((3,)), dma((3,)), dma((4,)), dma((4,)),
            dma((1,)), dma((1,)), dma((3, 8)), dma((3, 8)), dma, dma, dma, dma, dma((3,)),
            dma((6,)), dma((5,)), dma((5,)), dma, dma, dma((3,)),
        ],
        compiler_params=pltpu.CompilerParams(
            collective_id=0, has_side_effects=True, vmem_limit_bytes=60 * 1024 * 1024
        ),
    )(
        adjoint_end.reshape(4, 128, 128),
        face_courant,
        mixing,
        row_shift,
        tile_jac.reshape(4, 1024, 128),
        jnp.transpose(tile_cell[0], (0, 2, 1)),
        tile_count[0],
    )
    return out.reshape(4, 32, 4, 128), flux.reshape(4, 4, 128)


def solution(mesh):
    in_specs = (
        P(None, None, "lat", "lon"),
        P(None, None, None, "lat", "lon"),
        P(None, "lat", "lon"),
        P(None, "lat"),
        P(("lon", "lat"), None, None, None, None),
        P(("lon", "lat"), None, None, None),
        P(("lon", "lat"), None, None),
    )
    out_specs = (P(None, None, "lat", "lon"), P(None, "lat", "lon"))
    return jax.shard_map(shards, mesh=mesh, in_specs=in_specs, out_specs=out_specs, check_vma=False)
```

```python
import functools

import jax
import jax.numpy as jnp
from jax import lax
from jax.experimental import pallas as pl
from jax.experimental.pallas import tpu as pltpu
from jax.sharding import PartitionSpec as P

MESH = pl.DeviceIdType.MESH
F32 = jnp.float32
N_LON = 16
N_LAT = 8
N_DEV = N_LON * N_LAT
SHIFT_LANE = 32
ORDER = {
    "here": ("courant3", "send_rates", ),
    "wait3": ("turn2", "tiles2", "turn1", ),
    "sent1": ("send_cells", "tiles1", "pass_rates", "courant2", "turn0", "tiles0", ),
    "got1": ("courant1", ),
    "rolled3": ("wait_cells", "scatter2", ),
    "sentE2": ("scatter1", "wait_rates", "return_rates", ),
    "gotE2": (),
    "rolled2": (),
    "sentE1": ("scatter0", "pass_edges", ),
    "gotE1": (),
    "rolled1": (),
    "sentE0": (),
}

def lon_of_group(g):
    k = g // 2
    x_hi = k // 4
    z = k + x_hi * (7 - 2 * k)
    return z * 4 + x_hi * 2 + g % 2


def group_of_lon(lon):
    z = lon // 4
    k = z + (lon // 2) % 2 * (7 - 2 * z)
    return k * 2 + lon % 2


def remote(src, dst, send_sem, recv_sem, lon, lat):
    return pltpu.make_async_remote_copy(
        src_ref=src,
        dst_ref=dst,
        send_sem=send_sem,
        recv_sem=recv_sem,
        device_id=(lon, lat),
        device_id_type=MESH,
    )


def wait_bytes(ref, sem):
    pltpu.make_async_copy(ref, ref, sem).wait()


def kernel(
    adj_hbm, courant_hbm, mixing_hbm, shift_hbm, jac, cell_hbm, count_hbm,
    out, flux_out,
    adj, courant, mixing, own_shift, cell, count, note, raw, tiles_out, cells_out, cells_in, values_t, force,
    jac_in, note_in, shifts, forcing, padded, rates, mixed, edges, courant_out,
    inbox, halo, courant_in, rates_in, rates_t, state, twice, rolled, final, final_out, flux, flux_send,
    rates0_out, rates0, rate_ends_out, rate_ends, rate_edge_out, rate_edge_in, rate_edge,
    last, edge0_out, edge0, ends_out, ends, padded0, beside, flux_in,
    js, jr, ns, nr, ps, pr, ks, kr, rs, rr, es, er, os, orv, xs, xr, sm, ls, ws, wr, cs, cr, ts, here, zs, zr,
):
    lon, lat = lax.axis_index("lon"), lax.axis_index("lat")
    me = lon * N_LAT + lat
    g = group_of_lon(lon)
    north, south = lax.rem(lat + N_LAT - 1, N_LAT), lax.rem(lat + 1, N_LAT)
    lon_up, lon_down = lon_of_group(lax.rem(g + 1, N_LON)), lon_of_group(lax.rem(g + N_LON - 1, N_LON))

    loads = [
        pltpu.make_async_copy(src, dst, ls.at[i])
        for i, (src, dst) in enumerate(
            (
                (cell_hbm, cell), (count_hbm, count), (shift_hbm, own_shift),
                (courant_hbm, courant), (mixing_hbm, mixing), (adj_hbm, adj),
            )
        )
    ]
    for load in loads:
        load.start()

    barrier = pltpu.get_barrier_semaphore()

    def peer(k):
        k = lax.rem(k * 37, N_DEV)
        return lax.rem(lon + k // N_LAT, N_LON), lax.rem(lat + k % N_LAT, N_LAT)

    def greet_group(k, carry):
        pl.semaphore_signal(barrier, inc=1, device_id=(lax.rem(lon + k, N_LON), lat), device_id_type=MESH)
        return carry

    def greet_column(k, carry):
        pl.semaphore_signal(barrier, inc=1, device_id=(lon, lax.rem(lat + k, N_LAT)), device_id_type=MESH)
        return carry

    def greet_again(k, carry):
        pl.semaphore_signal(here, inc=1, device_id=(lon, lax.rem(lat + k, N_LAT)), device_id_type=MESH)
        return carry

    lax.fori_loop(1, N_LAT, greet_column, 0)
    lax.fori_loop(1, N_LON, greet_group, 0)

    for load in loads[:3]:
        load.wait()
    slots = lax.broadcasted_iota(jnp.int32, (8, 128), 0)
    lines = [jnp.where(slots < count[t : t + 1], cell[t], -1) for t in range(4)]
    lines += [jnp.full((1, 128), own_shift[i // 4, i % 4], jnp.int32) for i in range(16)]
    note[...] = jnp.transpose(jnp.concatenate(lines + [jnp.zeros((80, 128), jnp.int32)], axis=0))

    for t in (2, 1, 0):
        pltpu.make_async_copy(jac.at[t], raw.at[t], ts.at[t]).start()

    pl.semaphore_wait(barrier, N_LON + N_LAT - 2)
    lax.fori_loop(1, N_LAT, greet_again, 0)

    def send_tiles(t, notes):
        def body(k, carry):
            p_lon, p_lat = peer(k)
            owner = p_lon * N_LAT + p_lat
            if notes:
                remote(note.at[pl.ds(owner, 1)], note_in.at[pl.ds(me, 1)], ns, nr, p_lon, p_lat).start()
            remote(
                jac.at[t, pl.ds(owner * 8, 8)], jac_in.at[t, pl.ds(me * 8, 8)], js.at[t], jr.at[t], p_lon, p_lat
            ).start()
            return carry

        if notes:
            pltpu.make_async_copy(note.at[pl.ds(me, 1)], note_in.at[pl.ds(me, 1)], nr).start()
        pltpu.make_async_copy(jac.at[t, pl.ds(me * 8, 8)], jac_in.at[t, pl.ds(me * 8, 8)], jr.at[t]).start()
        lax.fori_loop(1, N_DEV, body, 0)

    def turn_tiles(t):
        pltpu.make_async_copy(jac.at[t], raw.at[t], ts.at[t]).wait()

        def body(p, carry):
            rows = [raw[t, pl.ds((d * N_LAT + p) * 8, 8)] for d in range(N_LON)]
            entries = jnp.transpose(jnp.concatenate(rows, axis=0))
            for c in range(4):
                tiles_out[t, p, pl.ds(c, 32, stride=4)] = entries[c * 32 : c * 32 + 32]
            return carry

        lax.fori_loop(0, N_LAT, body, 0)

    def send_turned(t):
        def body(k, carry):
            p_lon, p_lat = peer(k)
            remote(
                tiles_out.at[t, p_lat, pl.ds(group_of_lon(p_lon) * 8, 8)],
                jac_in.at[t, pl.ds(me * 8, 8)],
                js.at[t], jr.at[t], p_lon, p_lat,
            ).start()
            return carry

        pltpu.make_async_copy(
            tiles_out.at[t, lat, pl.ds(g * 8, 8)], jac_in.at[t, pl.ds(me * 8, 8)], jr.at[t]
        ).start()
        lax.fori_loop(1, N_DEV, body, 0)

    def send_cells():
        part = cells_out.at[pl.ds(0, 24)]
        slot = cells_in.at[pl.ds(lon * 24, 24)]
        pltpu.make_async_copy(part, slot, cr).start()
        to_groups(lambda to, target: remote(part, slot, cs, cr, target, lat).start())

    def scatter_loop(t):
        wait_bytes(jac_in.at[t], jr.at[t])
        for e in range(8):
            values_t[pl.ds(e * 128, 128)] = jnp.transpose(jac_in[t, pl.ds(e, 128, stride=8)])
        columns = lax.broadcasted_iota(jnp.int32, (128, 128), 0)

        def body(d, carry):
            left, right = [], []
            for slot in range(8):
                place = cells_in[pl.ds(d * 24 + t * 8 + slot, 1)]
                row, column = place >> 7, place & 127
                value = values_t[pl.ds(d * 8 + slot, 8, stride=128)]
                value = jnp.concatenate([jnp.where(row == r, value, 0.0) for r in range(4)], axis=0)
                high = value.astype(jnp.bfloat16)
                low = (value - high.astype(F32)).astype(jnp.bfloat16)
                left.append(jnp.concatenate([high, low], axis=0))
                right.append(jnp.where(columns == column, 1.0, 0.0).astype(jnp.bfloat16))
            total = lax.dot_general(
                jnp.concatenate(left, axis=1),
                jnp.concatenate(right, axis=1),
                (((1,), (1,)), ((), ())),
                preferred_element_type=F32,
            )
            force[t, pl.ds(d, 32, stride=16)] = total[:32] + total[32:]
            return carry

        lax.fori_loop(0, N_LON, body, 0)

    def to_groups(send):
        def body(k, carry):
            target = lax.rem(lon + k, N_LON)
            send(group_of_lon(target), target)
            return carry

        lax.fori_loop(1, N_LON, body, 0)

    def send_blocks(src, dst, send_sem, recv_sem):
        pltpu.make_async_copy(src.at[pl.ds(g * 32, 32)], dst.at[pl.ds(lon * 32, 32)], recv_sem).start()

        def one(to, target):
            remote(
                src.at[pl.ds(to * 32, 32)], dst.at[pl.ds(lon * 32, 32)], send_sem, recv_sem, target, lat
            ).start()

        to_groups(one)

    def convert_courant(t):
        for face in range(4):
            values = courant[face, t].astype(F32).reshape(128, 128)
            for to in range(N_LON):
                courant_out[t, pl.ds(to * 32 + face * 8, 8)] = values[to * 8 : to * 8 + 8]

    def scatter(t):
        cell_ids = lax.broadcasted_iota(jnp.int32, (512, 128), 0)
        total = jnp.zeros((512, 256), F32)
        for pair in range(4):
            hot, value = [], []
            for slot in (2 * pair, 2 * pair + 1):
                row = cells_out[t * 8 + slot : t * 8 + slot + 1]
                hot.append(jnp.where(cell_ids == row, 1.0, 0.0).astype(jnp.bfloat16))
                x = jac_in[t, pl.ds(slot, 128, stride=8)]
                high = x.astype(jnp.bfloat16)
                low = (x - high.astype(F32)).astype(jnp.bfloat16)
                value.append(jnp.concatenate([high, low], axis=1))
            total = total + jnp.dot(
                jnp.concatenate(hot, axis=1), jnp.concatenate(value, axis=0), preferred_element_type=F32
            )
        both = total[:, :128] + total[:, 128:]
        for row in range(4):
            by_entry = jnp.transpose(both[row * 128 : row * 128 + 128])
            for c in range(4):
                forcing[c, pl.ds(row, 32, stride=4)] = by_entry[c * 32 : c * 32 + 32]

    def send_rates():
        loads[4].wait()
        rates[...] = jnp.zeros_like(rates)
        rates[pl.ds(8, 124)] = mixing[...].astype(F32).reshape(124, 128)
        pltpu.make_async_copy(rates.at[pl.ds(8 + g * 8, 8)], rates_in.at[pl.ds(lon * 8, 8)], rr.at[0]).start()

        def one(to, target):
            remote(
                rates.at[pl.ds(8 + to * 8, 8)], rates_in.at[pl.ds(lon * 8, 8)], rs.at[0], rr.at[0], target, lat
            ).start()

        to_groups(one)

    rate_moves = [
        remote(rates_t.at[pl.ds(1, 4), 2], rates_t.at[pl.ds(1, 4), 0], ws.at[0], wr.at[0], lon_up, lat),
        remote(rates_t.at[1, pl.ds(1, 2)], rates_t.at[5, pl.ds(1, 2)], ws.at[1], wr.at[1], lon, north),
        remote(rates_t.at[4, pl.ds(1, 2)], rates_t.at[0, pl.ds(1, 2)], ws.at[2], wr.at[2], lon, south),
        remote(rates_t.at[1, 2], rates_t.at[5, 0], ws.at[3], wr.at[3], lon_up, north),
        remote(rates_t.at[4, 2], rates_t.at[0, 0], ws.at[4], wr.at[4], lon_up, south),
    ]

    def pass_rates():
        wait_bytes(rates_in, rr.at[0])
        for l in range(2):
            for row in range(4):
                n = l * 4 + row
                rates_t[row + 1, l + 1] = jnp.concatenate(
                    [rates_in[pl.ds(n, 8, stride=8)], rates_in[pl.ds(64 + n, 8, stride=8)]], axis=0
                )
        for move in rate_moves:
            move.start()

    def wait_rates():
        for move in rate_moves:
            move.wait_recv()

    def to_owners(x):
        return jnp.where(lane < 32, pltpu.roll(x, 15, 0), pltpu.roll(x, 1, 0))

    def return_rates():
        column_ends = jnp.zeros((16, 128), F32)
        for l in range(2):
            for row in range(4):
                n = l * 4 + row
                value = rates_t[row + 1, l + 1]
                twice[n, pl.ds(0, 16)] = value
                twice[n, pl.ds(16, 16)] = value
                value = take_rolled(twice, n, row_roll(0, row + 1))
                final[pl.ds(n * 16, 16)] = value
                same = lax.rem(lane, 8) == n
                column_ends = jnp.where(same & (lane < 32), jnp.broadcast_to(value[:, :1], (16, 128)), column_ends)
                column_ends = jnp.where(
                    same & (lane >= 32), jnp.broadcast_to(value[:, 127:], (16, 128)), column_ends
                )
        rate_ends_out[...] = to_owners(column_ends)
        for d in range(N_LON):
            rates0_out[pl.ds(d * 8, 8)] = final[pl.ds(d, 8, stride=16)]
        place = rates0.at[pl.ds(8 + g * 8, 8)]
        pltpu.make_async_copy(rates0_out.at[pl.ds(lon * 8, 8)], place, zr.at[3]).start()
        pltpu.make_async_copy(rate_ends_out.at[pl.ds(lon, 1)], rate_ends.at[pl.ds(g, 1)], zr.at[4]).start()

        def one(to, target):
            remote(rates0_out.at[pl.ds(target * 8, 8)], place, zs.at[3], zr.at[3], target, lat).start()
            remote(
                rate_ends_out.at[pl.ds(target, 1)], rate_ends.at[pl.ds(g, 1)], zs.at[4], zr.at[4], target, lat
            ).start()

        to_groups(one)

    edge_moves = [
        remote(rate_edge_out.at[0], rate_edge_in.at[1], zs.at[5], zr.at[5], lon, north),
        remote(rate_edge_out.at[1], rate_edge_in.at[0], zs.at[6], zr.at[6], lon, south),
    ]

    def pass_edges():
        wait_bytes(rates0.at[pl.ds(8, 128)], zr.at[3])
        wait_bytes(rate_ends, zr.at[4])
        rate_edge_out[0] = rates0[pl.ds(8, 32, stride=4)]
        rate_edge_out[1] = rates0[pl.ds(11, 32, stride=4)]
        for move in edge_moves:
            move.start()

    def take_edges():
        for move in edge_moves:
            move.wait()
        for i in range(2):
            for c in range(4):
                rate_edge[i, pl.ds(8 + c, 32, stride=4)] = rate_edge_in[i]

    none = jnp.zeros((8, 128), F32)
    for i in range(2):
        for at in (0, 136):
            rate_edge[i, pl.ds(at, 8)] = none
            edge0[i, pl.ds(at, 8)] = none
    for at in (0, 136):
        rates0[pl.ds(at, 8)] = none
        for c in range(4):
            last[c, pl.ds(at, 8)] = none
            padded0[c, pl.ds(at, 8)] = none

    lane = lax.broadcasted_iota(jnp.int32, (16, 128), 1)

    def do(slot):
        for name in ORDER[slot]:
            what, t = name[:-1], int(name[-1]) if name[-1].isdigit() else None
            if what == "courant":
                if t == 3:
                    loads[3].wait()
                convert_courant(t)
                send_blocks(courant_out.at[t], courant_in.at[t], ks.at[t], kr.at[t])
            elif what == "turn":
                turn_tiles(t)
            elif what == "tiles":
                send_turned(t)
            elif what == "scatter":
                scatter_loop(t)
            else:
                {"return_rates": return_rates, "pass_edges": pass_edges, "take_edges": take_edges, "send_rates": send_rates, "pass_rates": pass_rates, "wait_rates": wait_rates,
                 "send_cells": send_cells, "wait_cells": lambda: wait_bytes(cells_in, cr)}[name]()

    do("here")
    pl.semaphore_wait(here, N_LAT - 1)

    send_tiles(3, True)
    do("wait3")
    wait_bytes(note_in, nr)
    cells_out[...] = jnp.transpose(note_in[...])[:32]
    for i, row in enumerate((north, lat, south)):
        pltpu.make_async_copy(note_in.at[pl.ds(lon * N_LAT + row, 1)], shifts.at[pl.ds(i, 1)], sm.at[i]).start()
    wait_bytes(jac_in.at[3], jr.at[3])
    scatter(3)

    loads[5].wait()
    padded[...] = jnp.zeros_like(padded)
    for c in range(4):
        padded[c, pl.ds(8, 128)] = adj[c] + forcing[c]
        mid, above, below = padded[c, pl.ds(8, 128)], padded[c, pl.ds(12, 128)], padded[c, pl.ds(4, 128)]
        value = mid + rates[pl.ds(8, 128)] * (above - mid) - rates[pl.ds(4, 128)] * (mid - below)
        for to in range(N_LON):
            mixed[0, pl.ds(to * 32 + c * 8, 8)] = value[to * 8 : to * 8 + 8]
        padded[c, pl.ds(8, 128)] = value
        edges[0, pl.ds(c, 32, stride=4)] = padded[c, pl.ds(8, 32, stride=4)]
        edges[1, pl.ds(c, 32, stride=4)] = padded[c, pl.ds(11, 32, stride=4)]
    send_blocks(mixed.at[0], inbox.at[0], ps.at[0], pr.at[0])

    def send_edges(k, carry):
        target = lax.rem(lon + k, N_LON)
        to = group_of_lon(target)
        remote(
            edges.at[1, pl.ds(to * 8, 8)], halo.at[0, pl.ds(lon * 8, 8)], ps.at[1], pr.at[1], target, south
        ).start()
        remote(
            edges.at[0, pl.ds(to * 8, 8)], halo.at[1, pl.ds(lon * 8, 8)], ps.at[2], pr.at[2], target, north
        ).start()
        return carry

    lax.fori_loop(0, N_LON, send_edges, 0)

    do("sent1")

    flux[...] = jnp.zeros_like(flux)

    def loop_block(ref, at, first, stride):
        half = 8 * stride
        return jnp.concatenate(
            [ref[at, pl.ds(first, 8, stride=stride)], ref[at, pl.ds(first + half, 8, stride=stride)]], axis=0
        )

    def put_twice(i, value):
        twice[i, pl.ds(0, 16)] = value
        twice[i, pl.ds(16, 16)] = value

    def row_roll(t, row):
        i, j = (0, 3) if row == 0 else (2, 0) if row == 5 else (1, row - 1)
        shift = shifts[i, SHIFT_LANE + t * 4 + j]
        q, r = shift // 128, lax.rem(shift, 128)
        return q, lax.rem(128 - r, 128), lane < 128 - r

    def take_rolled(ref, i, roll):
        q, back, inside = roll
        first = pltpu.roll(ref[i, pl.ds(q, 16)], back, 1)
        second = pltpu.roll(ref[i, pl.ds(q + 1, 16)], back, 1)
        return jnp.where(inside, first, second)

    def roll_rows(t):
        for row in range(6):
            roll = row_roll(t, row)

            def body(n, carry, row=row, roll=roll):
                i = row * 8 + n
                value = take_rolled(twice, i, roll)
                if row == 0:
                    value = jnp.where(lat == 0, 0.0, value)
                if row == 5:
                    value = jnp.where(lat == N_LAT - 1, 0.0, value)
                rolled[pl.ds(i * 16, 16)] = value
                return carry

            lax.fori_loop(0, 8, body, 0, unroll=True)

    def transport(t, finish):
        def body(n, carry):
            l, row = n // 4, lax.rem(n, 4)
            faces = [
                jnp.concatenate(
                    [
                        courant_in[t, pl.ds(face * 8 + n, 8, stride=32)],
                        courant_in[t, pl.ds(256 + face * 8 + n, 8, stride=32)],
                    ],
                    axis=0,
                )
                for face in range(4)
            ]
            for c in range(4):
                i = (row + 1) * 8 + l * 4 + c
                x, up, down = [rolled[pl.ds((i + 8 * k) * 16, 16)] for k in (0, 1, -1)]
                e = pltpu.roll(x, 127, 1)
                east = jnp.where(lane == 127, pltpu.roll(e, 15, 0), e)
                w = pltpu.roll(x, 1, 1)
                west = jnp.where(lane == 0, pltpu.roll(w, 1, 0), w)
                value = (
                    x + faces[0] * (up - x) + faces[1] * (down - x) + faces[2] * (east - x) + faces[3] * (west - x)
                )
                finish(c, l, row, n, value)
            return carry

        lax.fori_loop(0, 8, body, 0, unroll=True)
        return None

    def add_forcing(t, e):
        def finish(c, l, row, n, value):
            at = pl.ds((c * 4 + row) * 16, 16)

            @pl.when(l == 0)
            def _():
                flux[at] = flux[at] + value

            value = value + force[t, pl.ds(((row * 2 + l) * 4 + c) * 16, 16)]
            if t > 0:
                state[e, row + 1, l + 1, c] = value
            else:
                put_twice((row + 1) * 8 + l * 4 + c, value)

        return finish

    def exchange(e):
        own, first, last = pl.ds(1, 4), 1, 4
        moves = []
        for dg, dl in ((1, 0), (-1, 0), (0, -1), (0, 1), (1, -1), (1, 1), (-1, -1), (-1, 1)):
            rows = own if dl == 0 else first if dl < 0 else last
            to_rows = own if dl == 0 else 5 if dl < 0 else 0
            levels = pl.ds(1, 2) if dg == 0 else 2 if dg > 0 else 1
            to_levels = pl.ds(1, 2) if dg == 0 else 0 if dg > 0 else 3
            i = len(moves)
            move = remote(
                state.at[e, rows, levels], state.at[e, to_rows, to_levels], es.at[e, i], er.at[e, i],
                lon if dg == 0 else lon_up if dg > 0 else lon_down,
                lat if dl == 0 else north if dl < 0 else south,
            )
            sends, gets = [], []
            if dg:
                sends.append(g < N_LON - 1 if dg > 0 else g > 0)
                gets.append(g > 0 if dg > 0 else g < N_LON - 1)
            if dl:
                sends.append(lat > 0 if dl < 0 else lat < N_LAT - 1)
                gets.append(lat < N_LAT - 1 if dl < 0 else lat > 0)
            moves.append((move, functools.reduce(jnp.logical_and, sends), functools.reduce(jnp.logical_and, gets)))
        return moves

    def start_moves(moves):
        for move, sends, _ in moves:
            pl.when(sends)(move.start)

    def wait_moves(moves):
        for move, _, gets in moves:
            pl.when(gets)(move.wait_recv)

    def end_moves(moves):
        for move, sends, _ in moves:
            pl.when(sends)(move.wait_send)

    @pl.when(g == 0)
    def _():
        for e in range(3):
            state[e, :, 0] = jnp.zeros_like(state[e, :, 0])

    @pl.when(g == N_LON - 1)
    def _():
        for e in range(3):
            state[e, :, 3] = jnp.zeros_like(state[e, :, 3])

    def mix_rows(e):
        for row in range(6):
            for l in range(2):
                low, high = rates_t[row, l], rates_t[row, l + 1]

                def body(c, carry, row=row, l=l, low=low, high=high):
                    mid = state[e, row, l + 1, c]
                    value = mid + high * (state[e, row, l + 2, c] - mid) - low * (mid - state[e, row, l, c])
                    put_twice(row * 8 + l * 4 + c, value)
                    return carry

                lax.fori_loop(0, 4, body, 0, unroll=True)

    wait_bytes(inbox.at[0], pr.at[0])
    wait_bytes(halo.at[0], pr.at[1])
    wait_bytes(halo.at[1], pr.at[2])
    do("got1")
    for i in range(3):
        wait_bytes(note_in.at[pl.ds(0, 1)], sm.at[i])
    for l in range(2):
        for c in range(4):
            put_twice(l * 4 + c, loop_block(halo, 0, l * 4 + c, 8))
            put_twice(40 + l * 4 + c, loop_block(halo, 1, l * 4 + c, 8))
            for row in range(4):
                put_twice((row + 1) * 8 + l * 4 + c, loop_block(inbox, 0, c * 8 + l * 4 + row, 32))
    roll_rows(3)
    wait_bytes(courant_in.at[3], kr.at[3])
    do("rolled3")
    transport(3, add_forcing(2, 0))
    moves = exchange(0)
    start_moves(moves)

    do("sentE2")

    for t in (2, 1):
        wait_moves(moves)
        do(f"gotE{t}")
        mix_rows(2 - t)
        roll_rows(t)
        wait_bytes(courant_in.at[t], kr.at[t])
        do(f"rolled{t}")
        transport(t, add_forcing(t - 1, 3 - t))
        end_moves(moves)
        if t == 2:
            moves = exchange(1)
            start_moves(moves)
            do("sentE1")

    column_ends = jnp.zeros((16, 128), F32)
    for row in range(1, 5):
        roll = row_roll(0, row)
        for l in range(2):
            for c in range(4):
                i, n = row * 8 + l * 4 + c, c * 8 + l * 4 + row - 1
                value = take_rolled(twice, i, roll)
                rolled[pl.ds(i * 16, 16)] = value
                final[pl.ds(n * 16, 16)] = value
                column_ends = jnp.where(lane == n, pltpu.roll(value, n, 1), column_ends)
                column_ends = jnp.where(lane == 32 + n, pltpu.roll(value, 33 + n, 1), column_ends)
    ends_out[...] = to_owners(column_ends)
    for d in range(N_LON):
        for c in range(4):
            final_out[d, c] = final[pl.ds(c * 128 + d, 8, stride=16)]
        edge0_out[0, pl.ds(d * 8, 8)] = rolled[pl.ds(128 + d, 8, stride=16)]
        edge0_out[1, pl.ds(d * 8, 8)] = rolled[pl.ds(512 + d, 8, stride=16)]
        flux_send[d] = flux[pl.ds(d, 16, stride=16)]
    mine = last.at[:, pl.ds(8 + g * 8, 8)]
    pltpu.make_async_copy(final_out.at[lon], mine, orv).start()
    pltpu.make_async_copy(ends_out.at[pl.ds(lon, 1)], ends.at[pl.ds(g, 1)], zr.at[0]).start()

    def send_last(k, carry):
        target = lax.rem(lon + k, N_LON)

        @pl.when(k > 0)
        def _():
            remote(final_out.at[target], mine, os, orv, target, lat).start()
            remote(
                ends_out.at[pl.ds(target, 1)], ends.at[pl.ds(g, 1)], zs.at[0], zr.at[0], target, lat
            ).start()

        part = pl.ds(target * 8, 8)
        place = pl.ds(8 + g * 8, 8)
        remote(edge0_out.at[0, part], edge0.at[1, place], zs.at[1], zr.at[1], target, north).start()
        remote(edge0_out.at[1, part], edge0.at[0, place], zs.at[2], zr.at[2], target, south).start()
        return carry

    lax.fori_loop(0, N_LON, send_last, 0)

    @pl.when(g == 0)
    def _():
        pltpu.make_async_copy(flux_send.at[lon], flux_in, xr).start()

        def send_flux(k, carry):
            target = lax.rem(lon + k, N_LON)
            remote(flux_send.at[target], flux_in, xs, xr, target, lat).start()
            return carry

        lax.fori_loop(1, N_LON, send_flux, 0)
        wait_bytes(flux_send.at[pl.ds(0, N_LON - 1)], xs)

    def mix_padded(ref, rate):
        mid, above, below = ref[pl.ds(8, 128)], ref[pl.ds(12, 128)], ref[pl.ds(4, 128)]
        return mid + rate[pl.ds(8, 128)] * (above - mid) - rate[pl.ds(4, 128)] * (mid - below)

    take_edges()
    wait_bytes(ends, zr.at[0])
    upper = lax.rem(lane // 4, 2) == 1

    def next_level(x):
        return jnp.where(upper, pltpu.roll(pltpu.roll(x, 4, 1), 15, 0), pltpu.roll(x, 124, 1))

    def level_before(x):
        return jnp.where(upper, pltpu.roll(x, 4, 1), pltpu.roll(pltpu.roll(x, 124, 1), 1, 0))

    x, rate = ends[...], rate_ends[...]
    x = x + rate * (next_level(x) - x) - level_before(rate) * (x - level_before(x))
    x = jnp.transpose(x)
    for i in range(2):
        wait_bytes(edge0.at[i, pl.ds(8, 128)], zr.at[1 if i == 1 else 2])
        value = mix_padded(edge0.at[i], rate_edge.at[i])
        value = jnp.where(lat == (0 if i == 0 else N_LAT - 1), 0.0, value)
        padded0[0, pl.ds(8, 128)] = value
        for c in range(4):
            beside[i, c, pl.ds(3 * i, 32, stride=4)] = padded0[0, pl.ds(8 + c, 32, stride=4)]
    wait_bytes(last.at[:, pl.ds(8, 128)], orv)
    for c in range(4):
        padded0[c, pl.ds(8, 128)] = mix_padded(last.at[c], rates0)
    faces = [courant[face, 0].astype(F32).reshape(128, 128) for face in range(4)]
    cell_row = lax.rem(lax.broadcasted_iota(jnp.int32, (128, 128), 0), 4)
    cell_column = lax.broadcasted_iota(jnp.int32, (128, 128), 1)
    wait_bytes(flux_in, xr)
    for c in range(4):
        mid = padded0[c, pl.ds(8, 128)]
        up = jnp.where(cell_row == 3, beside[1, c], padded0[c, pl.ds(9, 128)])
        down = jnp.where(cell_row == 0, beside[0, c], padded0[c, pl.ds(7, 128)])
        right, left = [
            jnp.concatenate(
                [
                    jnp.broadcast_to(x[first + c * 8 : first + c * 8 + 8, k : k + 1], (8, 128))
                    for k in range(N_LON)
                ],
                axis=0,
            )
            for first in (0, 32)
        ]
        east = jnp.where(cell_column == 127, right, pltpu.roll(mid, 127, 1))
        west = jnp.where(cell_column == 0, left, pltpu.roll(mid, 1, 1))
        value = (
            mid + faces[0] * (up - mid) + faces[1] * (down - mid) + faces[2] * (east - mid) + faces[3] * (west - mid)
        )
        out[c] = value
        flux_out[pl.ds(c * 4, 4)] = flux_in[pl.ds(c * 4, 4)] + value[:4]

    for t in range(4):
        wait_bytes(jac_in.at[t, pl.ds(0, 8 * (N_DEV - 1))], js.at[t])
    wait_bytes(note_in.at[pl.ds(0, N_DEV - 1)], ns)
    wait_bytes(cells_in.at[pl.ds(0, 24 * (N_LON - 1))], cs)
    wait_bytes(inbox.at[0, pl.ds(0, 480)], ps.at[0])
    wait_bytes(halo.at[0], ps.at[1])
    wait_bytes(halo.at[1], ps.at[2])
    for t in range(1, 4):
        wait_bytes(courant_in.at[t, pl.ds(0, 480)], ks.at[t])
    wait_bytes(rates_in.at[pl.ds(0, 120)], rs.at[0])
    for move in rate_moves:
        move.wait_send()
    wait_bytes(final_out.at[pl.ds(0, N_LON - 1)], os)
    wait_bytes(ends_out.at[pl.ds(0, N_LON - 1)], zs.at[0])
    wait_bytes(edge0_out.at[0], zs.at[1])
    wait_bytes(edge0_out.at[1], zs.at[2])
    wait_bytes(rates0_out.at[pl.ds(0, 120)], zs.at[3])
    wait_bytes(rate_ends_out.at[pl.ds(0, N_LON - 1)], zs.at[4])


def hand_over(field, flux, field_out, flux_out):
    field_out[...] = field[...]
    flux_out[...] = flux[...]


def shards(adjoint_end, face_courant, mixing, row_shift, tile_jac, tile_cell, tile_count):
    dma = pltpu.SemaphoreType.DMA
    vmem = pltpu.VMEM
    whole = pl.BlockSpec(memory_space=pltpu.VMEM)
    out, flux = pl.pallas_call(
        kernel,
        out_shape=(
            jax.ShapeDtypeStruct((4, 128, 128), F32),
            jax.ShapeDtypeStruct((16, 128), F32),
        ),
        in_specs=[pl.BlockSpec(memory_space=pl.ANY)] * 7,
        out_specs=(whole, whole),
        scratch_shapes=[
            vmem((4, 128, 128), F32),
            vmem((4, 4, 32, 4, 128), jnp.bfloat16),
            vmem((31, 4, 128), jnp.bfloat16),
            pltpu.SMEM((4, 4), jnp.int32),
            vmem((4, 8, 128), jnp.int32),
            vmem((4, 128), jnp.int32),
            vmem((128, 128), jnp.int32),
            vmem((3, 1024, 128), F32),
            vmem((3, 8, 128, 128), F32),
            vmem((32, 128), jnp.int32),
            vmem((384, 128), jnp.int32),
            vmem((1024, 128), F32),
            vmem((3, 512, 128), F32),
            vmem((4, 1024, 128), F32),
            vmem((128, 128), jnp.int32),
            pltpu.SMEM((3, 128), jnp.int32),
            vmem((4, 128, 128), F32),
            vmem((4, 144, 128), F32),
            vmem((144, 128), F32),
            vmem((1, 512, 128), F32),
            vmem((2, 128, 128), F32),
            vmem((4, 512, 128), F32),
            vmem((1, 512, 128), F32),
            vmem((2, 128, 128), F32),
            vmem((4, 512, 128), F32),
            vmem((128, 128), F32),
            vmem((6, 3, 16, 128), F32),
            vmem((3, 6, 4, 4, 16, 128), F32),
            vmem((48, 32, 128), F32),
            vmem((768, 128), F32),
            vmem((512, 128), F32),
            vmem((16, 4, 8, 128), F32),
            vmem((256, 128), F32),
            vmem((16, 16, 128), F32),
            vmem((128, 128), F32),
            vmem((144, 128), F32),
            vmem((16, 128), F32),
            vmem((16, 128), F32),
            vmem((2, 32, 128), F32),
            vmem((2, 32, 128), F32),
            vmem((2, 144, 128), F32),
            vmem((4, 144, 128), F32),
            vmem((2, 128, 128), F32),
            vmem((2, 144, 128), F32),
            vmem((16, 128), F32),
            vmem((16, 128), F32),
            vmem((4, 144, 128), F32),
            vmem((2, 4, 128, 128), F32),
            vmem((16, 128), F32),
            dma((4,)), dma((4,)), dma, dma, dma((3,)), dma((3,)), dma((4,)), dma((4,)),
            dma((1,)), dma((1,)), dma((3, 8)), dma((3, 8)), dma, dma, dma, dma, dma((3,)),
            dma((6,)), dma((5,)), dma((5,)), dma, dma, dma((3,)), pltpu.SemaphoreType.REGULAR, dma((7,)), dma((7,)),
        ],
        compiler_params=pltpu.CompilerParams(
            collective_id=0, has_side_effects=True, vmem_limit_bytes=60 * 1024 * 1024
        ),
    )(
        adjoint_end.reshape(4, 128, 128),
        face_courant,
        mixing,
        row_shift,
        tile_jac.reshape(4, 1024, 128),
        jnp.transpose(tile_cell[0], (0, 2, 1)),
        tile_count[0],
    )
    out, flux = pl.pallas_call(
        hand_over,
        out_shape=(jax.ShapeDtypeStruct((4, 128, 128), F32), jax.ShapeDtypeStruct((16, 128), F32)),
        in_specs=[whole, whole],
        out_specs=(whole, whole),
    )(out, flux)
    return out.reshape(4, 32, 4, 128), flux.reshape(4, 4, 128)


def solution(mesh):
    in_specs = (
        P(None, None, "lat", "lon"),
        P(None, None, None, "lat", "lon"),
        P(None, "lat", "lon"),
        P(None, "lat"),
        P(("lon", "lat"), None, None, None, None),
        P(("lon", "lat"), None, None, None),
        P(("lon", "lat"), None, None),
    )
    out_specs = (P(None, None, "lat", "lon"), P(None, "lat", "lon"))
    return jax.shard_map(shards, mesh=mesh, in_specs=in_specs, out_specs=out_specs, check_vma=False)
```

```python
import functools

import jax
import jax.numpy as jnp
from jax import lax
from jax.experimental import pallas as pl
from jax.experimental.pallas import tpu as pltpu
from jax.sharding import PartitionSpec as P

MESH = pl.DeviceIdType.MESH
F32 = jnp.float32
N_LON = 16
N_LAT = 8
N_DEV = N_LON * N_LAT
SHIFT_LANE = 32
ORDER = {
    "greeted": ("make_note", ),
    "here": ("courant3", "send_rates", ),
    "wait3": ("send_notes", "turn2", "tiles2", "turn1", ),
    "noted": ("send_cells", ),
    "sent1": ("tiles1", "courant2", "pass_cells", "pass_rates", "turn0", "wait_cells", "scatter2", ),
    "got1": (),
    "rolled3": (),
    "sentE2": ("tiles0", "courant1", "scatter1", "wait_rates", "return_rates", ),
    "gotE2": (),
    "rolled2": (),
    "sentE1": ("scatter0", "pass_edges", ),
    "gotE1": (),
    "rolled1": (),
    "sentE0": (),
}

def lon_of_group(g):
    k = g // 2
    x_hi = k // 4
    z = k + x_hi * (7 - 2 * k)
    return z * 4 + x_hi * 2 + g % 2


def group_of_lon(lon):
    z = lon // 4
    k = z + (lon // 2) % 2 * (7 - 2 * z)
    return k * 2 + lon % 2


def remote(src, dst, send_sem, recv_sem, lon, lat):
    return pltpu.make_async_remote_copy(
        src_ref=src,
        dst_ref=dst,
        send_sem=send_sem,
        recv_sem=recv_sem,
        device_id=(lon, lat),
        device_id_type=MESH,
    )


def wait_bytes(ref, sem):
    pltpu.make_async_copy(ref, ref, sem).wait()


def kernel(
    adj_hbm, courant_hbm, mixing_hbm, shift_hbm, jac, cell_hbm, count_hbm,
    out, flux_out,
    adj, courant, mixing, own_shift, cell, count, note, raw, tiles_out, cells_out, cells_in, values_t, force,
    jac_in, note_in, shifts, forcing, padded, rates, mixed, edges, courant_out,
    inbox, halo, courant_in, rates_in, rates_t, state, twice, rolled, final, final_out, flux, flux_send,
    rates0_out, rates0, rate_ends_out, rate_ends, rate_edge_out, rate_edge_in, rate_edge,
    last, edge0_out, edge0, ends_out, ends, padded0, beside, flux_in,
    js, jr, ns, nr, ps, pr, ks, kr, rs, rr, es, er, os, orv, xs, xr, sm, ls, ws, wr, cs, cr, ts, here, zs, zr,
):
    lon, lat = lax.axis_index("lon"), lax.axis_index("lat")
    me = lon * N_LAT + lat
    g = group_of_lon(lon)
    north, south = lax.rem(lat + N_LAT - 1, N_LAT), lax.rem(lat + 1, N_LAT)
    lon_up, lon_down = lon_of_group(lax.rem(g + 1, N_LON)), lon_of_group(lax.rem(g + N_LON - 1, N_LON))

    loads = [
        pltpu.make_async_copy(src, dst, ls.at[i])
        for i, (src, dst) in enumerate(
            (
                (cell_hbm, cell), (count_hbm, count), (shift_hbm, own_shift),
                (courant_hbm, courant), (mixing_hbm, mixing), (adj_hbm, adj),
            )
        )
    ]
    for load in loads:
        load.start()

    barrier = pltpu.get_barrier_semaphore()

    def peer(k):
        k = lax.rem(k * 37, N_DEV)
        return lax.rem(lon + k // N_LAT, N_LON), lax.rem(lat + k % N_LAT, N_LAT)

    def greet_group(k, carry):
        pl.semaphore_signal(barrier, inc=1, device_id=(lax.rem(lon + k, N_LON), lat), device_id_type=MESH)
        return carry

    def greet_column(k, carry):
        pl.semaphore_signal(barrier, inc=1, device_id=(lon, lax.rem(lat + k, N_LAT)), device_id_type=MESH)
        return carry

    def greet_again(k, carry):
        pl.semaphore_signal(here, inc=1, device_id=(lon, lax.rem(lat + k, N_LAT)), device_id_type=MESH)
        return carry

    lax.fori_loop(1, N_LAT, greet_column, 0)
    lax.fori_loop(1, N_LON, greet_group, 0)


    def make_note():
        for load in loads[:3]:
            load.wait()
        slots = lax.broadcasted_iota(jnp.int32, (8, 128), 0)
        lines = [jnp.where(slots < count[t : t + 1], cell[t], -1) for t in range(4)]
        lines += [jnp.full((1, 128), own_shift[i // 4, i % 4], jnp.int32) for i in range(16)]
        note[...] = jnp.transpose(jnp.concatenate(lines + [jnp.zeros((80, 128), jnp.int32)], axis=0))

    def send_notes():
        def body(k, carry):
            p_lon, p_lat = peer(k)
            remote(
                note.at[pl.ds(p_lon * N_LAT + p_lat, 1)], note_in.at[pl.ds(me, 1)], ns, nr, p_lon, p_lat
            ).start()
            return carry

        pltpu.make_async_copy(note.at[pl.ds(me, 1)], note_in.at[pl.ds(me, 1)], nr).start()
        lax.fori_loop(1, N_DEV, body, 0)

    def send_tiles(t):
        def body(k, carry):
            p_lon, p_lat = peer(k)
            owner = p_lon * N_LAT + p_lat
            remote(
                jac.at[t, pl.ds(owner * 8, 8)], jac_in.at[t, pl.ds(me * 8, 8)], js.at[t], jr.at[t], p_lon, p_lat
            ).start()
            return carry

        pltpu.make_async_copy(jac.at[t, pl.ds(me * 8, 8)], jac_in.at[t, pl.ds(me * 8, 8)], jr.at[t]).start()
        lax.fori_loop(1, N_DEV, body, 0)

    def turn_tiles(t):
        pltpu.make_async_copy(jac.at[t], raw.at[t], ts.at[t]).wait()

        def body(p, carry):
            rows = [raw[t, pl.ds((d * N_LAT + p) * 8, 8)] for d in range(N_LON)]
            entries = jnp.transpose(jnp.concatenate(rows, axis=0))
            for c in range(4):
                tiles_out[t, p, pl.ds(c, 32, stride=4)] = entries[c * 32 : c * 32 + 32]
            return carry

        lax.fori_loop(0, N_LAT, body, 0)

    def send_turned(t):
        def body(k, carry):
            p_lon, p_lat = peer(k)
            remote(
                tiles_out.at[t, p_lat, pl.ds(group_of_lon(p_lon) * 8, 8)],
                jac_in.at[t, pl.ds(me * 8, 8)],
                js.at[t], jr.at[t], p_lon, p_lat,
            ).start()
            return carry

        pltpu.make_async_copy(
            tiles_out.at[t, lat, pl.ds(g * 8, 8)], jac_in.at[t, pl.ds(me * 8, 8)], jr.at[t]
        ).start()
        lax.fori_loop(1, N_DEV, body, 0)

    core = lax.rem(lon, 2)

    def send_cells():
        part = cells_out.at[pl.ds(0, 24)]
        slot = cells_in.at[pl.ds(core * 192 + lon // 2 * 24, 24)]
        pltpu.make_async_copy(part, slot, cr.at[0]).start()

        def body(k, carry):
            remote(part, slot, cs.at[0], cr.at[0], lax.rem(lon + 2 * k, N_LON), lat).start()
            return carry

        lax.fori_loop(1, N_LON // 2, body, 0)

    def core_cells():
        half = cells_in.at[pl.ds(core * 192, 192)]
        return remote(half, half, cs.at[1], cr.at[1], lon + 1 - 2 * core, lat)

    def pass_cells():
        wait_bytes(cells_in.at[pl.ds(core * 192, 192)], cr.at[0])
        core_cells().start()

    def scatter_loop(t):
        wait_bytes(jac_in.at[t], jr.at[t])
        for e in range(8):
            values_t[pl.ds(e * 128, 128)] = jnp.transpose(jac_in[t, pl.ds(e, 128, stride=8)])
        columns = lax.broadcasted_iota(jnp.int32, (128, 128), 0)

        def body(d, carry):
            left, right = [], []
            for slot in range(8):
                place = cells_in[pl.ds(lax.rem(d, 2) * 192 + d // 2 * 24 + t * 8 + slot, 1)]
                row, column = place >> 7, place & 127
                value = values_t[pl.ds(d * 8 + slot, 8, stride=128)]
                value = jnp.concatenate([jnp.where(row == r, value, 0.0) for r in range(4)], axis=0)
                high = value.astype(jnp.bfloat16)
                low = (value - high.astype(F32)).astype(jnp.bfloat16)
                left.append(jnp.concatenate([high, low], axis=0))
                right.append(jnp.where(columns == column, 1.0, 0.0).astype(jnp.bfloat16))
            total = lax.dot_general(
                jnp.concatenate(left, axis=1),
                jnp.concatenate(right, axis=1),
                (((1,), (1,)), ((), ())),
                preferred_element_type=F32,
            )
            force[t, pl.ds(d, 32, stride=16)] = total[:32] + total[32:]
            return carry

        lax.fori_loop(0, N_LON, body, 0)

    def to_groups(send):
        def body(k, carry):
            target = lax.rem(lon + k, N_LON)
            send(group_of_lon(target), target)
            return carry

        lax.fori_loop(1, N_LON, body, 0)

    def send_blocks(src, dst, send_sem, recv_sem):
        pltpu.make_async_copy(src.at[pl.ds(g * 32, 32)], dst.at[pl.ds(lon * 32, 32)], recv_sem).start()

        def one(to, target):
            remote(
                src.at[pl.ds(to * 32, 32)], dst.at[pl.ds(lon * 32, 32)], send_sem, recv_sem, target, lat
            ).start()

        to_groups(one)

    def convert_courant(t):
        for face in range(4):
            values = courant[face, t].astype(F32).reshape(128, 128)
            for to in range(N_LON):
                courant_out[t, pl.ds(to * 32 + face * 8, 8)] = values[to * 8 : to * 8 + 8]

    def scatter(t):
        cell_ids = lax.broadcasted_iota(jnp.int32, (512, 128), 0)
        total = jnp.zeros((512, 256), F32)
        for pair in range(4):
            hot, value = [], []
            for slot in (2 * pair, 2 * pair + 1):
                row = cells_out[t * 8 + slot : t * 8 + slot + 1]
                hot.append(jnp.where(cell_ids == row, 1.0, 0.0).astype(jnp.bfloat16))
                x = jac_in[t, pl.ds(slot, 128, stride=8)]
                high = x.astype(jnp.bfloat16)
                low = (x - high.astype(F32)).astype(jnp.bfloat16)
                value.append(jnp.concatenate([high, low], axis=1))
            total = total + jnp.dot(
                jnp.concatenate(hot, axis=1), jnp.concatenate(value, axis=0), preferred_element_type=F32
            )
        both = total[:, :128] + total[:, 128:]
        for row in range(4):
            by_entry = jnp.transpose(both[row * 128 : row * 128 + 128])
            for c in range(4):
                forcing[c, pl.ds(row, 32, stride=4)] = by_entry[c * 32 : c * 32 + 32]

    def send_rates():
        loads[4].wait()
        rates[...] = jnp.zeros_like(rates)
        rates[pl.ds(8, 124)] = mixing[...].astype(F32).reshape(124, 128)
        pltpu.make_async_copy(rates.at[pl.ds(8 + g * 8, 8)], rates_in.at[pl.ds(lon * 8, 8)], rr.at[0]).start()

        def one(to, target):
            remote(
                rates.at[pl.ds(8 + to * 8, 8)], rates_in.at[pl.ds(lon * 8, 8)], rs.at[0], rr.at[0], target, lat
            ).start()

        to_groups(one)

    rate_moves = [
        remote(rates_t.at[pl.ds(1, 4), 2], rates_t.at[pl.ds(1, 4), 0], ws.at[0], wr.at[0], lon_up, lat),
        remote(rates_t.at[1, pl.ds(1, 2)], rates_t.at[5, pl.ds(1, 2)], ws.at[1], wr.at[1], lon, north),
        remote(rates_t.at[4, pl.ds(1, 2)], rates_t.at[0, pl.ds(1, 2)], ws.at[2], wr.at[2], lon, south),
        remote(rates_t.at[1, 2], rates_t.at[5, 0], ws.at[3], wr.at[3], lon_up, north),
        remote(rates_t.at[4, 2], rates_t.at[0, 0], ws.at[4], wr.at[4], lon_up, south),
    ]

    def pass_rates():
        wait_bytes(rates_in, rr.at[0])
        for l in range(2):
            for row in range(4):
                n = l * 4 + row
                rates_t[row + 1, l + 1] = jnp.concatenate(
                    [rates_in[pl.ds(n, 8, stride=8)], rates_in[pl.ds(64 + n, 8, stride=8)]], axis=0
                )
        for move in rate_moves:
            move.start()

    def wait_rates():
        for move in rate_moves:
            move.wait_recv()

    def to_owners(x):
        return jnp.where(lane < 32, pltpu.roll(x, 15, 0), pltpu.roll(x, 1, 0))

    def return_rates():
        column_ends = jnp.zeros((16, 128), F32)
        for l in range(2):
            for row in range(4):
                n = l * 4 + row
                value = rates_t[row + 1, l + 1]
                twice[n, pl.ds(0, 16)] = value
                twice[n, pl.ds(16, 16)] = value
                value = take_rolled(twice, n, row_roll(0, row + 1))
                final[pl.ds(n * 16, 16)] = value
                same = lax.rem(lane, 8) == n
                column_ends = jnp.where(same & (lane < 32), jnp.broadcast_to(value[:, :1], (16, 128)), column_ends)
                column_ends = jnp.where(
                    same & (lane >= 32), jnp.broadcast_to(value[:, 127:], (16, 128)), column_ends
                )
        rate_ends_out[...] = to_owners(column_ends)
        for d in range(N_LON):
            rates0_out[pl.ds(d * 8, 8)] = final[pl.ds(d, 8, stride=16)]
        place = rates0.at[pl.ds(8 + g * 8, 8)]
        pltpu.make_async_copy(rates0_out.at[pl.ds(lon * 8, 8)], place, zr.at[3]).start()
        pltpu.make_async_copy(rate_ends_out.at[pl.ds(lon, 1)], rate_ends.at[pl.ds(g, 1)], zr.at[4]).start()

        def one(to, target):
            remote(rates0_out.at[pl.ds(target * 8, 8)], place, zs.at[3], zr.at[3], target, lat).start()
            remote(
                rate_ends_out.at[pl.ds(target, 1)], rate_ends.at[pl.ds(g, 1)], zs.at[4], zr.at[4], target, lat
            ).start()

        to_groups(one)

    edge_moves = [
        remote(rate_edge_out.at[0], rate_edge_in.at[1], zs.at[5], zr.at[5], lon, north),
        remote(rate_edge_out.at[1], rate_edge_in.at[0], zs.at[6], zr.at[6], lon, south),
    ]

    def pass_edges():
        wait_bytes(rates0.at[pl.ds(8, 128)], zr.at[3])
        wait_bytes(rate_ends, zr.at[4])
        rate_edge_out[0] = rates0[pl.ds(8, 32, stride=4)]
        rate_edge_out[1] = rates0[pl.ds(11, 32, stride=4)]
        for move in edge_moves:
            move.start()

    def take_edges():
        for move in edge_moves:
            move.wait()
        for i in range(2):
            for c in range(4):
                rate_edge[i, pl.ds(8 + c, 32, stride=4)] = rate_edge_in[i]

    none = jnp.zeros((8, 128), F32)
    for i in range(2):
        for at in (0, 136):
            rate_edge[i, pl.ds(at, 8)] = none
            edge0[i, pl.ds(at, 8)] = none
    for at in (0, 136):
        rates0[pl.ds(at, 8)] = none
        for c in range(4):
            last[c, pl.ds(at, 8)] = none
            padded0[c, pl.ds(at, 8)] = none

    lane = lax.broadcasted_iota(jnp.int32, (16, 128), 1)

    def do(slot):
        for name in ORDER[slot]:
            what, t = name[:-1], int(name[-1]) if name[-1].isdigit() else None
            if what == "courant":
                if t == 3:
                    loads[3].wait()
                convert_courant(t)
                send_blocks(courant_out.at[t], courant_in.at[t], ks.at[t], kr.at[t])
            elif what == "turn":
                turn_tiles(t)
            elif what == "tiles":
                send_turned(t)
            elif what == "scatter":
                scatter_loop(t)
            else:
                {"make_note": make_note, "send_notes": send_notes, "return_rates": return_rates, "pass_edges": pass_edges, "take_edges": take_edges, "send_rates": send_rates, "pass_rates": pass_rates, "wait_rates": wait_rates,
                 "send_cells": send_cells, "pass_cells": pass_cells, "wait_cells": lambda: core_cells().wait_recv()}[name]()

    do("greeted")

    for t in (2, 1, 0):
        pltpu.make_async_copy(jac.at[t], raw.at[t], ts.at[t]).start()

    pl.semaphore_wait(barrier, N_LON + N_LAT - 2)
    lax.fori_loop(1, N_LAT, greet_again, 0)
    do("here")
    pl.semaphore_wait(here, N_LAT - 1)

    send_tiles(3)
    do("wait3")
    wait_bytes(note_in, nr)
    cells_out[...] = jnp.transpose(note_in[...])[:32]
    do("noted")
    for i, row in enumerate((north, lat, south)):
        pltpu.make_async_copy(note_in.at[pl.ds(lon * N_LAT + row, 1)], shifts.at[pl.ds(i, 1)], sm.at[i]).start()
    wait_bytes(jac_in.at[3], jr.at[3])
    scatter(3)

    loads[5].wait()
    padded[...] = jnp.zeros_like(padded)
    for c in range(4):
        padded[c, pl.ds(8, 128)] = adj[c] + forcing[c]
        mid, above, below = padded[c, pl.ds(8, 128)], padded[c, pl.ds(12, 128)], padded[c, pl.ds(4, 128)]
        value = mid + rates[pl.ds(8, 128)] * (above - mid) - rates[pl.ds(4, 128)] * (mid - below)
        for to in range(N_LON):
            mixed[0, pl.ds(to * 32 + c * 8, 8)] = value[to * 8 : to * 8 + 8]
        padded[c, pl.ds(8, 128)] = value
        edges[0, pl.ds(c, 32, stride=4)] = padded[c, pl.ds(8, 32, stride=4)]
        edges[1, pl.ds(c, 32, stride=4)] = padded[c, pl.ds(11, 32, stride=4)]
    send_blocks(mixed.at[0], inbox.at[0], ps.at[0], pr.at[0])

    def send_edges(k, carry):
        target = lax.rem(lon + k, N_LON)
        to = group_of_lon(target)
        remote(
            edges.at[1, pl.ds(to * 8, 8)], halo.at[0, pl.ds(lon * 8, 8)], ps.at[1], pr.at[1], target, south
        ).start()
        remote(
            edges.at[0, pl.ds(to * 8, 8)], halo.at[1, pl.ds(lon * 8, 8)], ps.at[2], pr.at[2], target, north
        ).start()
        return carry

    lax.fori_loop(0, N_LON, send_edges, 0)

    do("sent1")

    flux[...] = jnp.zeros_like(flux)

    def loop_block(ref, at, first, stride):
        half = 8 * stride
        return jnp.concatenate(
            [ref[at, pl.ds(first, 8, stride=stride)], ref[at, pl.ds(first + half, 8, stride=stride)]], axis=0
        )

    def put_twice(i, value):
        twice[i, pl.ds(0, 16)] = value
        twice[i, pl.ds(16, 16)] = value

    def row_roll(t, row):
        i, j = (0, 3) if row == 0 else (2, 0) if row == 5 else (1, row - 1)
        shift = shifts[i, SHIFT_LANE + t * 4 + j]
        q, r = shift // 128, lax.rem(shift, 128)
        return q, lax.rem(128 - r, 128), lane < 128 - r

    def take_rolled(ref, i, roll):
        q, back, inside = roll
        first = pltpu.roll(ref[i, pl.ds(q, 16)], back, 1)
        second = pltpu.roll(ref[i, pl.ds(q + 1, 16)], back, 1)
        return jnp.where(inside, first, second)

    def roll_rows(t):
        for row in range(6):
            roll = row_roll(t, row)

            def body(n, carry, row=row, roll=roll):
                i = row * 8 + n
                value = take_rolled(twice, i, roll)
                if row == 0:
                    value = jnp.where(lat == 0, 0.0, value)
                if row == 5:
                    value = jnp.where(lat == N_LAT - 1, 0.0, value)
                rolled[pl.ds(i * 16, 16)] = value
                return carry

            lax.fori_loop(0, 8, body, 0, unroll=True)

    def transport(t, finish):
        def body(n, carry):
            l, row = n // 4, lax.rem(n, 4)
            faces = [
                jnp.concatenate(
                    [
                        courant_in[t, pl.ds(face * 8 + n, 8, stride=32)],
                        courant_in[t, pl.ds(256 + face * 8 + n, 8, stride=32)],
                    ],
                    axis=0,
                )
                for face in range(4)
            ]
            for c in range(4):
                i = (row + 1) * 8 + l * 4 + c
                x, up, down = [rolled[pl.ds((i + 8 * k) * 16, 16)] for k in (0, 1, -1)]
                e = pltpu.roll(x, 127, 1)
                east = jnp.where(lane == 127, pltpu.roll(e, 15, 0), e)
                w = pltpu.roll(x, 1, 1)
                west = jnp.where(lane == 0, pltpu.roll(w, 1, 0), w)
                value = (
                    x + faces[0] * (up - x) + faces[1] * (down - x) + faces[2] * (east - x) + faces[3] * (west - x)
                )
                finish(c, l, row, n, value)
            return carry

        lax.fori_loop(0, 8, body, 0, unroll=True)
        return None

    def add_forcing(t, e):
        def finish(c, l, row, n, value):
            at = pl.ds((c * 4 + row) * 16, 16)

            @pl.when(l == 0)
            def _():
                flux[at] = flux[at] + value

            value = value + force[t, pl.ds(((row * 2 + l) * 4 + c) * 16, 16)]
            if t > 0:
                state[e, row + 1, l + 1, c] = value
            else:
                put_twice((row + 1) * 8 + l * 4 + c, value)

        return finish

    def exchange(e):
        own, first, last = pl.ds(1, 4), 1, 4
        moves = []
        for dg, dl in ((1, 0), (-1, 0), (0, -1), (0, 1), (1, -1), (1, 1), (-1, -1), (-1, 1)):
            rows = own if dl == 0 else first if dl < 0 else last
            to_rows = own if dl == 0 else 5 if dl < 0 else 0
            levels = pl.ds(1, 2) if dg == 0 else 2 if dg > 0 else 1
            to_levels = pl.ds(1, 2) if dg == 0 else 0 if dg > 0 else 3
            i = len(moves)
            move = remote(
                state.at[e, rows, levels], state.at[e, to_rows, to_levels], es.at[e, i], er.at[e, i],
                lon if dg == 0 else lon_up if dg > 0 else lon_down,
                lat if dl == 0 else north if dl < 0 else south,
            )
            sends, gets = [], []
            if dg:
                sends.append(g < N_LON - 1 if dg > 0 else g > 0)
                gets.append(g > 0 if dg > 0 else g < N_LON - 1)
            if dl:
                sends.append(lat > 0 if dl < 0 else lat < N_LAT - 1)
                gets.append(lat < N_LAT - 1 if dl < 0 else lat > 0)
            moves.append((move, functools.reduce(jnp.logical_and, sends), functools.reduce(jnp.logical_and, gets)))
        return moves

    def start_moves(moves):
        for move, sends, _ in moves:
            pl.when(sends)(move.start)

    def wait_moves(moves):
        for move, _, gets in moves:
            pl.when(gets)(move.wait_recv)

    def end_moves(moves):
        for move, sends, _ in moves:
            pl.when(sends)(move.wait_send)

    @pl.when(g == 0)
    def _():
        for e in range(3):
            state[e, :, 0] = jnp.zeros_like(state[e, :, 0])

    @pl.when(g == N_LON - 1)
    def _():
        for e in range(3):
            state[e, :, 3] = jnp.zeros_like(state[e, :, 3])

    def mix_rows(e):
        for row in range(6):
            for l in range(2):
                low, high = rates_t[row, l], rates_t[row, l + 1]

                def body(c, carry, row=row, l=l, low=low, high=high):
                    mid = state[e, row, l + 1, c]
                    value = mid + high * (state[e, row, l + 2, c] - mid) - low * (mid - state[e, row, l, c])
                    put_twice(row * 8 + l * 4 + c, value)
                    return carry

                lax.fori_loop(0, 4, body, 0, unroll=True)

    wait_bytes(inbox.at[0], pr.at[0])
    wait_bytes(halo.at[0], pr.at[1])
    wait_bytes(halo.at[1], pr.at[2])
    do("got1")
    for i in range(3):
        wait_bytes(note_in.at[pl.ds(0, 1)], sm.at[i])
    for l in range(2):
        for c in range(4):
            put_twice(l * 4 + c, loop_block(halo, 0, l * 4 + c, 8))
            put_twice(40 + l * 4 + c, loop_block(halo, 1, l * 4 + c, 8))
            for row in range(4):
                put_twice((row + 1) * 8 + l * 4 + c, loop_block(inbox, 0, c * 8 + l * 4 + row, 32))
    roll_rows(3)
    wait_bytes(courant_in.at[3], kr.at[3])
    do("rolled3")
    transport(3, add_forcing(2, 0))
    moves = exchange(0)
    start_moves(moves)

    do("sentE2")

    for t in (2, 1):
        wait_moves(moves)
        do(f"gotE{t}")
        mix_rows(2 - t)
        roll_rows(t)
        wait_bytes(courant_in.at[t], kr.at[t])
        do(f"rolled{t}")
        transport(t, add_forcing(t - 1, 3 - t))
        end_moves(moves)
        if t == 2:
            moves = exchange(1)
            start_moves(moves)
            do("sentE1")

    column_ends = jnp.zeros((16, 128), F32)
    for row in range(1, 5):
        roll = row_roll(0, row)
        for l in range(2):
            for c in range(4):
                i, n = row * 8 + l * 4 + c, c * 8 + l * 4 + row - 1
                value = take_rolled(twice, i, roll)
                rolled[pl.ds(i * 16, 16)] = value
                final[pl.ds(n * 16, 16)] = value
                column_ends = jnp.where(lane == n, pltpu.roll(value, n, 1), column_ends)
                column_ends = jnp.where(lane == 32 + n, pltpu.roll(value, 33 + n, 1), column_ends)
    ends_out[...] = to_owners(column_ends)
    for d in range(N_LON):
        for c in range(4):
            final_out[d, c] = final[pl.ds(c * 128 + d, 8, stride=16)]
        edge0_out[0, pl.ds(d * 8, 8)] = rolled[pl.ds(128 + d, 8, stride=16)]
        edge0_out[1, pl.ds(d * 8, 8)] = rolled[pl.ds(512 + d, 8, stride=16)]
        flux_send[d] = flux[pl.ds(d, 16, stride=16)]
    mine = last.at[:, pl.ds(8 + g * 8, 8)]
    pltpu.make_async_copy(final_out.at[lon], mine, orv).start()
    pltpu.make_async_copy(ends_out.at[pl.ds(lon, 1)], ends.at[pl.ds(g, 1)], zr.at[0]).start()

    def send_last(k, carry):
        target = lax.rem(lon + k, N_LON)

        @pl.when(k > 0)
        def _():
            remote(final_out.at[target], mine, os, orv, target, lat).start()
            remote(
                ends_out.at[pl.ds(target, 1)], ends.at[pl.ds(g, 1)], zs.at[0], zr.at[0], target, lat
            ).start()

        part = pl.ds(target * 8, 8)
        place = pl.ds(8 + g * 8, 8)
        remote(edge0_out.at[0, part], edge0.at[1, place], zs.at[1], zr.at[1], target, north).start()
        remote(edge0_out.at[1, part], edge0.at[0, place], zs.at[2], zr.at[2], target, south).start()
        return carry

    lax.fori_loop(0, N_LON, send_last, 0)

    @pl.when(g == 0)
    def _():
        pltpu.make_async_copy(flux_send.at[lon], flux_in, xr).start()

        def send_flux(k, carry):
            target = lax.rem(lon + k, N_LON)
            remote(flux_send.at[target], flux_in, xs, xr, target, lat).start()
            return carry

        lax.fori_loop(1, N_LON, send_flux, 0)
        wait_bytes(flux_send.at[pl.ds(0, N_LON - 1)], xs)

    def mix_padded(ref, rate):
        mid, above, below = ref[pl.ds(8, 128)], ref[pl.ds(12, 128)], ref[pl.ds(4, 128)]
        return mid + rate[pl.ds(8, 128)] * (above - mid) - rate[pl.ds(4, 128)] * (mid - below)

    take_edges()
    wait_bytes(ends, zr.at[0])
    upper = lax.rem(lane // 4, 2) == 1

    def next_level(x):
        return jnp.where(upper, pltpu.roll(pltpu.roll(x, 4, 1), 15, 0), pltpu.roll(x, 124, 1))

    def level_before(x):
        return jnp.where(upper, pltpu.roll(x, 4, 1), pltpu.roll(pltpu.roll(x, 124, 1), 1, 0))

    x, rate = ends[...], rate_ends[...]
    x = x + rate * (next_level(x) - x) - level_before(rate) * (x - level_before(x))
    x = jnp.transpose(x)
    for i in range(2):
        wait_bytes(edge0.at[i, pl.ds(8, 128)], zr.at[1 if i == 1 else 2])
        value = mix_padded(edge0.at[i], rate_edge.at[i])
        value = jnp.where(lat == (0 if i == 0 else N_LAT - 1), 0.0, value)
        padded0[0, pl.ds(8, 128)] = value
        for c in range(4):
            beside[i, c, pl.ds(3 * i, 32, stride=4)] = padded0[0, pl.ds(8 + c, 32, stride=4)]
    wait_bytes(last.at[:, pl.ds(8, 128)], orv)
    for c in range(4):
        padded0[c, pl.ds(8, 128)] = mix_padded(last.at[c], rates0)
    faces = [courant[face, 0].astype(F32).reshape(128, 128) for face in range(4)]
    cell_row = lax.rem(lax.broadcasted_iota(jnp.int32, (128, 128), 0), 4)
    cell_column = lax.broadcasted_iota(jnp.int32, (128, 128), 1)
    wait_bytes(flux_in, xr)
    for c in range(4):
        mid = padded0[c, pl.ds(8, 128)]
        up = jnp.where(cell_row == 3, beside[1, c], padded0[c, pl.ds(9, 128)])
        down = jnp.where(cell_row == 0, beside[0, c], padded0[c, pl.ds(7, 128)])
        right, left = [
            jnp.concatenate(
                [
                    jnp.broadcast_to(x[first + c * 8 : first + c * 8 + 8, k : k + 1], (8, 128))
                    for k in range(N_LON)
                ],
                axis=0,
            )
            for first in (0, 32)
        ]
        east = jnp.where(cell_column == 127, right, pltpu.roll(mid, 127, 1))
        west = jnp.where(cell_column == 0, left, pltpu.roll(mid, 1, 1))
        value = (
            mid + faces[0] * (up - mid) + faces[1] * (down - mid) + faces[2] * (east - mid) + faces[3] * (west - mid)
        )
        out[c] = value
        flux_out[pl.ds(c * 4, 4)] = flux_in[pl.ds(c * 4, 4)] + value[:4]

    for t in range(4):
        wait_bytes(jac_in.at[t, pl.ds(0, 8 * (N_DEV - 1))], js.at[t])
    wait_bytes(note_in.at[pl.ds(0, N_DEV - 1)], ns)
    wait_bytes(cells_in.at[pl.ds(0, 24 * 7)], cs.at[0])
    core_cells().wait_send()
    wait_bytes(inbox.at[0, pl.ds(0, 480)], ps.at[0])
    wait_bytes(halo.at[0], ps.at[1])
    wait_bytes(halo.at[1], ps.at[2])
    for t in range(1, 4):
        wait_bytes(courant_in.at[t, pl.ds(0, 480)], ks.at[t])
    wait_bytes(rates_in.at[pl.ds(0, 120)], rs.at[0])
    for move in rate_moves:
        move.wait_send()
    wait_bytes(final_out.at[pl.ds(0, N_LON - 1)], os)
    wait_bytes(ends_out.at[pl.ds(0, N_LON - 1)], zs.at[0])
    wait_bytes(edge0_out.at[0], zs.at[1])
    wait_bytes(edge0_out.at[1], zs.at[2])
    wait_bytes(rates0_out.at[pl.ds(0, 120)], zs.at[3])
    wait_bytes(rate_ends_out.at[pl.ds(0, N_LON - 1)], zs.at[4])


def hand_over(field, flux, field_out, flux_out):
    field_out[...] = field[...]
    flux_out[...] = flux[...]


def shards(adjoint_end, face_courant, mixing, row_shift, tile_jac, tile_cell, tile_count):
    dma = pltpu.SemaphoreType.DMA
    vmem = pltpu.VMEM
    whole = pl.BlockSpec(memory_space=pltpu.VMEM)
    out, flux = pl.pallas_call(
        kernel,
        out_shape=(
            jax.ShapeDtypeStruct((4, 128, 128), F32),
            jax.ShapeDtypeStruct((16, 128), F32),
        ),
        in_specs=[pl.BlockSpec(memory_space=pl.ANY)] * 7,
        out_specs=(whole, whole),
        scratch_shapes=[
            vmem((4, 128, 128), F32),
            vmem((4, 4, 32, 4, 128), jnp.bfloat16),
            vmem((31, 4, 128), jnp.bfloat16),
            pltpu.SMEM((4, 4), jnp.int32),
            vmem((4, 8, 128), jnp.int32),
            vmem((4, 128), jnp.int32),
            vmem((128, 128), jnp.int32),
            vmem((3, 1024, 128), F32),
            vmem((3, 8, 128, 128), F32),
            vmem((32, 128), jnp.int32),
            vmem((384, 128), jnp.int32),
            vmem((1024, 128), F32),
            vmem((3, 512, 128), F32),
            vmem((4, 1024, 128), F32),
            vmem((128, 128), jnp.int32),
            pltpu.SMEM((3, 128), jnp.int32),
            vmem((4, 128, 128), F32),
            vmem((4, 144, 128), F32),
            vmem((144, 128), F32),
            vmem((1, 512, 128), F32),
            vmem((2, 128, 128), F32),
            vmem((4, 512, 128), F32),
            vmem((1, 512, 128), F32),
            vmem((2, 128, 128), F32),
            vmem((4, 512, 128), F32),
            vmem((128, 128), F32),
            vmem((6, 3, 16, 128), F32),
            vmem((3, 6, 4, 4, 16, 128), F32),
            vmem((48, 32, 128), F32),
            vmem((768, 128), F32),
            vmem((512, 128), F32),
            vmem((16, 4, 8, 128), F32),
            vmem((256, 128), F32),
            vmem((16, 16, 128), F32),
            vmem((128, 128), F32),
            vmem((144, 128), F32),
            vmem((16, 128), F32),
            vmem((16, 128), F32),
            vmem((2, 32, 128), F32),
            vmem((2, 32, 128), F32),
            vmem((2, 144, 128), F32),
            vmem((4, 144, 128), F32),
            vmem((2, 128, 128), F32),
            vmem((2, 144, 128), F32),
            vmem((16, 128), F32),
            vmem((16, 128), F32),
            vmem((4, 144, 128), F32),
            vmem((2, 4, 128, 128), F32),
            vmem((16, 128), F32),
            dma((4,)), dma((4,)), dma, dma, dma((3,)), dma((3,)), dma((4,)), dma((4,)),
            dma((1,)), dma((1,)), dma((3, 8)), dma((3, 8)), dma, dma, dma, dma, dma((3,)),
            dma((6,)), dma((5,)), dma((5,)), dma((2,)), dma((2,)), dma((3,)), pltpu.SemaphoreType.REGULAR, dma((7,)), dma((7,)),
        ],
        compiler_params=pltpu.CompilerParams(
            collective_id=0, has_side_effects=True, vmem_limit_bytes=60 * 1024 * 1024
        ),
    )(
        adjoint_end.reshape(4, 128, 128),
        face_courant,
        mixing,
        row_shift,
        tile_jac.reshape(4, 1024, 128),
        jnp.transpose(tile_cell[0], (0, 2, 1)),
        tile_count[0],
    )
    out, flux = pl.pallas_call(
        hand_over,
        out_shape=(jax.ShapeDtypeStruct((4, 128, 128), F32), jax.ShapeDtypeStruct((16, 128), F32)),
        in_specs=[whole, whole],
        out_specs=(whole, whole),
    )(out, flux)
    return out.reshape(4, 32, 4, 128), flux.reshape(4, 4, 128)


def solution(mesh):
    in_specs = (
        P(None, None, "lat", "lon"),
        P(None, None, None, "lat", "lon"),
        P(None, "lat", "lon"),
        P(None, "lat"),
        P(("lon", "lat"), None, None, None, None),
        P(("lon", "lat"), None, None, None),
        P(("lon", "lat"), None, None),
    )
    out_specs = (P(None, None, "lat", "lon"), P(None, "lat", "lon"))
    return jax.shard_map(shards, mesh=mesh, in_specs=in_specs, out_specs=out_specs, check_vma=False)
```
